512 devices in a mesh: aux: 64 (over z, y), bas: 8 (over x, core).
Axes of the slice: x: 4, y: 8, z: 8, core: 2. Of those that a mesh axis runs over, the one named last changes fastest.
Arguments:
- integrals: bfloat16 [64, 48, 16, 128, 128], P('aux', 'bas'), may hold values from -6 to 6
- coefficients: bfloat16 [6144, 1024], P(('aux', 'bas')), may hold values from -0.125 to 0.125
- metric: bfloat16 [64, 64], replicated, may hold values from -0.75 to 0.75
- pair_blocks: int32 [48, 16], P('bas'), may hold values from 0 to 47, as said below
- pair_live: int32 [48, 16], P('bas'), may hold values 0 or 1
Outputs:
- exchange_rows: float32 [512, 6144], P('aux', 'bas')
The draws below stay inside these ranges and needn't reach their ends.
Inputs may be any that keep to these rules, and one draw needn't show every extreme that they name: `pair_blocks`: within one row the 16 block numbers are different.
All inputs are finite; a program needn't handle non-finite values. No bound on the sum of `pair_live` on one device may be relied on, other than what follows from the above.
Results may differ from the reference program's by a relative error of at most 0.0024.
Values may be sent and summed in bfloat16 or wider, within the bound.
A program may use at most 128 MiB of HBM per device.

```python
import math
import jax
import jax.numpy as jnp
from jax import lax

NB = 6144
BS = 128
NZ = 16
OCC = 1024
KROWS = 512
NAUX = 64
NBLK = 48


def draw_pair_blocks(key, part):
    block_count = NB // BS
    scores = jax.random.randint(key, (block_count, block_count), 0, 4096) * block_count + jnp.arange(block_count, dtype=jnp.int32)[None, :]
    order = jnp.argsort(scores, axis=1, stable=True)
    return order[:, :NZ].astype(jnp.int32)


def plant(entries, own_key, least, top_value):
    longest = entries.shape.index(max(entries.shape))
    spots = []
    for shift in (0, 1):
        where = [jax.random.randint(jax.random.fold_in(own_key, axis), (), 0, length) for axis, length in enumerate(entries.shape)]
        where[longest] = (where[longest] + shift) % entries.shape[longest]
        spots.append(tuple(where))
    return entries.at[spots[0]].set(least).at[spots[1]].set(top_value)


def block_scale(key, extent, cuts, low, high):
    def one(position, blocks):
        steps = jax.random.uniform(jax.random.fold_in(jax.random.fold_in(key, 6), position), (blocks,), jnp.float32, low / len(cuts), high / len(cuts))
        return jnp.repeat(jnp.exp(steps), extent[position] // blocks).reshape((-1,) + (1,) * (len(extent) - position - 1))

    loudness = one(*cuts[0])
    for cut in cuts[1:]:
        loudness = loudness * one(*cut)
    return loudness


def centred(own_key, shape, scale, most, shards=(), kind=jnp.bfloat16):
    entries = jax.random.normal(own_key, shape, jnp.float32) * scale
    if len(shards) > 0:
        entries = block_scale(own_key, shape, shards, -0.22, 0.18) * entries
    return jnp.clip(entries, min=-most, max=most).astype(kind)


def setup_inputs(seed: int = 0) -> dict:
    arg_keys = jax.random.split(jax.random.key(seed), 6)
    return {
        "integrals": centred(arg_keys[0], (NAUX, NBLK, NZ, BS, BS), 1.0, 6.0, ((0, 64), (1, 8))),
        "coefficients": centred(arg_keys[1], (NB, OCC), (BS * NZ) ** -0.5, 0.125, ((0, 512),)),
        "metric": centred(arg_keys[2], (NAUX, NAUX), NAUX ** -0.5, 0.75),
        "pair_blocks": draw_pair_blocks(jax.random.fold_in(arg_keys[5], 71), 0),
        "pair_live": plant((jax.random.randint(arg_keys[4], (NBLK, NZ), 0, 4) < 3).astype(jnp.int32), jax.random.fold_in(arg_keys[4], 1), 0, 1),
    }


def reference(integrals, coefficients, metric, pair_blocks, pair_live):
    block_count = NB // BS
    coeff_tiles = coefficients.reshape(block_count, BS, OCC)

    def one_block(pieces):
        ints_row, lam_row, live_row = pieces
        picked = coeff_tiles[lam_row.astype(jnp.int32)].astype(jnp.float32) * live_row.astype(jnp.float32)[:, None, None]
        done = jnp.einsum('pzab,zbo->poa', ints_row.astype(jnp.float32), picked)
        return done.astype(jnp.bfloat16)
    half_done = lax.map(one_block, (jnp.moveaxis(integrals, 1, 0), pair_blocks, pair_live))
    half_done = jnp.transpose(half_done, (1, 2, 0, 3)).reshape(NAUX, OCC * NB)
    regrouped = jnp.dot(metric, half_done, preferred_element_type=jnp.float32).astype(jnp.bfloat16)
    regrouped = regrouped.reshape(NAUX * OCC, NB)
    window = regrouped[:, :KROWS]
    exchange_part = jnp.dot(window.T, regrouped, preferred_element_type=jnp.float32)
    return exchange_part * (1.0 / math.sqrt(NAUX * OCC))
```

```python
import functools
import math

import jax
import jax.numpy as jnp
from jax import lax
from jax.experimental import pallas as pl
from jax.experimental.pallas import tpu as pltpu
from jax.sharding import PartitionSpec as P

BF16 = jnp.bfloat16
F32 = jnp.float32
GROUPS = 4
GRAN = 32


def kernel(
    dims,
    ints_hbm,
    coef_ref,
    metric_ref,
    tab_smem,
    tab_vmem,
    out_ref,
    ints,
    raw_f32,
    raw_send,
    raw_recv,
    join_f32,
    coeff,
    kron,
    win,
    win_tiles,
    mid_a,
    mixin,
    mixed,
    mid_b,
    imix_tiles,
    imix,
    tab_land,
    tab_win,
    wfull,
    half,
    exch,
    send_a,
    recv_a,
    send_b,
    recv_b,
    send_a2,
    recv_a2,
    send_b2,
    recv_b2,
    local_sem,
    raw_ssem,
    raw_rsem,
    scat_ssem,
    scat_rsem,
    ph2_ssem,
    ph2_rsem,
    ring_ssem,
    ring_rsem,
    sib_ssem,
    sib_rsem,
    a2a_ssem,
    a2a_rsem,
    w_ssem,
    w_rsem,
    ws_ssem,
    ws_rsem,
    rs_ssem,
    rs_rsem,
):
    zn, yn, xn, bs, nz, nrow, occ, krows, rows_dev, nb = dims
    bas_n = 2 * xn
    aux_n = zn * yn
    block = rows_dev * bas_n
    gcol = occ // GROUPS
    ms = krows // bas_n
    out_rows = krows // aux_n
    ncol = nrow * bs
    hcol = ncol // 2
    dead = nb // bs

    aux = lax.axis_index("aux")
    bas = lax.axis_index("bas")
    z, y = aux // yn, lax.rem(aux, yn)
    x, c = bas // 2, lax.rem(bas, 2)
    sib = (aux, x * 2 + 1 - c)

    def at_y(k):
        return (z * yn + lax.rem(y + k, yn), bas)

    def at_z(k):
        return (lax.rem(z + k, zn) * yn + y, bas)

    def at_bas(k):
        return (aux, lax.rem(bas + k, bas_n))

    def at_x(k):
        return (aux, lax.rem(x + k, xn) * 2 + c)

    def remote(src, dst, ssem, rsem, dev):
        return pltpu.make_async_remote_copy(
            src_ref=src, dst_ref=dst, send_sem=ssem, recv_sem=rsem,
            device_id=dev, device_id_type=pl.DeviceIdType.MESH)

    barrier = pltpu.get_barrier_semaphore()
    for k in range(1, yn):
        pl.semaphore_signal(barrier, inc=1, device_id=at_y(k), device_id_type=pl.DeviceIdType.MESH)
    for k in range(1, zn):
        pl.semaphore_signal(barrier, inc=1, device_id=at_z(k), device_id_type=pl.DeviceIdType.MESH)
    for k in range(1, bas_n):
        pl.semaphore_signal(barrier, inc=1, device_id=at_bas(k), device_id_type=pl.DeviceIdType.MESH)

    fetch = pltpu.make_async_copy(ints_hbm, ints, local_sem.at[0])
    fetch.start()
    raw_f32[...] = jnp.zeros_like(raw_f32)
    raw_f32[0:rows_dev, :] = coef_ref[...].astype(F32)
    packed = raw_f32[...].astype(BF16)
    raw_send[0] = packed[:, : occ // 2]
    raw_send[1] = packed[:, occ // 2 :]
    pl.semaphore_wait(barrier, yn - 1 + zn - 1 + bas_n - 1)

    def raw_copy(k):
        to = lax.rem(bas + k, bas_n)
        return remote(raw_send.at[lax.rem(to, 2)], raw_recv.at[bas], raw_ssem.at[k], raw_rsem.at[k], (aux, to))

    for k in range(1, bas_n):
        raw_copy(k).start()
    raw_recv[bas] = raw_send[c]

    def win_src(j):
        b = (j * ms) // bs
        off = (j * ms) % bs
        return ints_hbm.at[b, :, pl.ds(off, ms), :]

    @pl.when(bas == 0)
    def _():
        for j in range(1, bas_n):
            remote(tab_vmem, tab_land, scat_ssem.at[j, 1], scat_rsem.at[1], (aux, j)).start()
            remote(win_src(j), win, scat_ssem.at[j, 0], scat_rsem.at[0], (aux, j)).start()
        pltpu.make_async_copy(tab_vmem, tab_land, local_sem.at[2]).start()
        pltpu.make_async_copy(win_src(0), win, local_sem.at[1]).start()

    metric = metric_ref[...]
    gram = lax.dot_general(metric, metric, (((0,), (0,)), ((), ())), preferred_element_type=F32).astype(BF16)
    krow = yn * 16
    spread_c = (
        lax.broadcasted_iota(jnp.int32, (aux_n, aux_n * 16), 0)
        == (lax.broadcasted_iota(jnp.int32, (aux_n, aux_n * 16), 1) >> 4)
    ).astype(F32).astype(BF16)

    def kron_step(t, carry):
        r0 = pl.multiple_of(t * krow, krow)
        spread_r = (
            ((lax.broadcasted_iota(jnp.int32, (krow, aux_n), 0) + r0) >> 4)
            == lax.broadcasted_iota(jnp.int32, (krow, aux_n), 1)
        ).astype(F32).astype(BF16)
        rows = jnp.dot(spread_r, gram, preferred_element_type=F32).astype(BF16)
        full = jnp.dot(rows, spread_c, preferred_element_type=F32)
        same = (lax.broadcasted_iota(jnp.int32, full.shape, 0) & 15) == (
            lax.broadcasted_iota(jnp.int32, full.shape, 1) & 15)
        kron[pl.ds(r0, krow), :] = jnp.where(same, full, 0.0).astype(BF16)
        return carry

    lax.fori_loop(0, aux_n * 16 // krow, kron_step, 0)
    for g in range(GROUPS):
        coeff[g, nb // GRAN : (nb + bs) // GRAN] = jnp.zeros((bs // GRAN, GRAN, gcol), BF16)

    for k in range(1, bas_n):
        raw_copy(k).wait()
    for j in range(bas_n):
        join_f32[j * rows_dev : (j + 1) * rows_dev, :] = raw_recv[j][0:rows_dev, :].astype(F32)
    joined = join_f32[...].astype(BF16)
    per = block // GRAN
    coeff[2 * c, pl.ds(aux * per, per)] = joined[:, :gcol].reshape(per, GRAN, gcol)
    coeff[2 * c + 1, pl.ds(aux * per, per)] = joined[:, gcol:].reshape(per, GRAN, gcol)

    def at_block(st, zz, yy):
        return coeff.at[2 * c + st, pl.ds((zz * yn + yy) * per, per)]

    def ph2_copy(st, k):
        ref = at_block(st, z, y)
        return remote(ref, ref, ph2_ssem.at[st, k], ph2_rsem.at[st, k], at_z(k) if st == 0 else at_y(k))

    for k in range(1, max(zn, yn)):
        if k < zn:
            ph2_copy(0, k).start()
        if k < yn:
            ph2_copy(1, k).start()

    def slab_block(st, pos, q):
        return at_block(st, q, pos) if st == 0 else at_block(st, pos, q)

    def ring_copy(st, q, s):
        n, me, at = (yn, y, at_y) if st == 0 else (zn, z, at_z)
        m = zn if st == 0 else yn
        if isinstance(q, int):
            right = 1 if q < m // 2 else n - 1
        else:
            right = jnp.where(q < m // 2, 1, n - 1)
        pos = lax.rem(me + s * (n - right), n)
        ref = slab_block(st, pos, q)
        return remote(ref, ref, ring_ssem.at[st, q, s], ring_rsem.at[st, q, s], at(right))

    def sib_copy(st, q, s):
        n, me = (yn, y) if st == 0 else (zn, z)
        m = zn if st == 0 else yn
        if isinstance(q, int):
            right = 1 if q < m // 2 else n - 1
        else:
            right = jnp.where(q < m // 2, 1, n - 1)
        ref = slab_block(st, lax.rem(me + s * (n - right), n), q)
        return remote(ref, ref, sib_ssem.at[st, q, s], sib_rsem.at[st, q, s], sib)

    every = [(st, q) for i in range(max(zn, yn) // 2) for st in range(2)
             for q in (i, i + (zn if st == 0 else yn) // 2)]
    steps = yn - 1

    def ring_step(s, carry):
        for st, q in every:
            ring_copy(st, q, s).wait_recv()
            ring_copy(st, q, s + 1).start()
            sib_copy(st, q, s + 1).start()
        return carry

    def a2a_y(i, src, mid, k):
        to = lax.rem(y + k, yn)
        return remote(src.at[:, to], mid.at[y], a2a_ssem.at[i, 0, k], a2a_rsem.at[i, 0, k], at_y(k))

    def a2a_z(i, mid, dst, k):
        to = lax.rem(z + k, zn)
        return remote(mid.at[:, to], dst.at[z], a2a_ssem.at[i, 1, k], a2a_rsem.at[i, 1, k], at_z(k))

    def a2a_y_start(i, src, mid):
        for k in range(1, yn):
            a2a_y(i, src, mid, k).start()
        mid[y] = src[:, y]

    def a2a_z_start(i, src, mid, dst):
        for k in range(1, yn):
            a2a_y(i, src, mid, k).wait()
        for k in range(1, zn):
            a2a_z(i, mid, dst, k).start()
        dst[z] = mid[:, z]

    def a2a_end(i, mid, dst):
        for k in range(1, zn):
            a2a_z(i, mid, dst, k).wait()

    @pl.when(bas == 0)
    def _():
        pltpu.make_async_copy(tab_vmem, tab_land, local_sem.at[2]).wait()
        pltpu.make_async_copy(win_src(0), win, local_sem.at[1]).wait()

    @pl.when(bas != 0)
    def _():
        remote(tab_vmem, tab_land, scat_ssem.at[0, 1], scat_rsem.at[1], (aux, 0)).wait_recv()
        remote(win_src(0), win, scat_ssem.at[0, 0], scat_rsem.at[0], (aux, 0)).wait_recv()

    win_tiles[...] = win[...].reshape(zn, yn, 16, bs)
    a2a_y_start(0, win_tiles, mid_a)
    to_smem = pltpu.make_async_copy(tab_land, tab_win, local_sem.at[3])
    to_smem.start()

    for st, q0 in ((0, z), (1, y)):
        ring_copy(st, q0, 0).start()
        sib_copy(st, q0, 0).start()
    for k in range(1, max(zn, yn)):
        for st, q0, n in ((0, z, zn), (1, y, yn)):
            if k < n:
                ph2_copy(st, k).wait_recv()
                q = lax.rem(q0 + n - k, n)
                ring_copy(st, q, 0).start()
                sib_copy(st, q, 0).start()

    cut = [min(steps - 1, i) for i in (1, 2, 3, 4)]
    lax.fori_loop(0, cut[0], ring_step, 0)
    a2a_z_start(0, win_tiles, mid_a, mixin)
    lax.fori_loop(cut[0], cut[1], ring_step, 0)
    a2a_end(0, mid_a, mixin)

    def mix_step(t, carry):
        r0 = pl.multiple_of(t * krow, krow)
        rows = jnp.dot(
            kron[pl.ds(r0, krow), :], mixin[...].reshape(aux_n * 16, bs), preferred_element_type=F32)
        mixed[t] = rows.astype(BF16).reshape(yn, 16, bs)
        return carry

    lax.fori_loop(0, zn, mix_step, 0)
    a2a_y_start(1, mixed, mid_b)
    lax.fori_loop(cut[1], cut[2], ring_step, 0)
    a2a_z_start(1, mixed, mid_b, imix_tiles)
    lax.fori_loop(cut[2], steps - 1, ring_step, 0)
    a2a_end(1, mid_b, imix_tiles)
    imix[...] = imix_tiles[...].reshape(nz, ms, bs)
    for st, q in every:
        ring_copy(st, q, steps - 1).wait_recv()
        sib_copy(st, q, steps).start()
    fetch.wait()
    to_smem.wait()
    def sib_wait(s, carry):
        for st, q in every:
            sib_copy(st, q, s).wait_recv()
        return carry

    lax.fori_loop(0, steps + 1, sib_wait, 0)

    def block_of(g, index):
        return coeff[g, pl.ds(index * (bs // GRAN), bs // GRAN)].reshape(bs, gcol)

    wrow = (bas * ms) // bs

    def w_step(g, carry):
        acc = jnp.zeros((ms, gcol), F32)
        for s in range(0, nz, 2):
            lhs = jnp.concatenate([imix[s], imix[s + 1]], axis=1)
            rhs = jnp.concatenate([block_of(g, tab_win[wrow, s]), block_of(g, tab_win[wrow, s + 1])], axis=0)
            acc = acc + jnp.dot(lhs, rhs, preferred_element_type=F32)
        wfull[g, pl.ds(pl.multiple_of(bas * ms, 16), ms), :] = acc.astype(BF16)
        return carry

    lax.fori_loop(0, GROUPS, w_step, 0)

    def w_rows(j):
        return wfull.at[:, pl.ds(pl.multiple_of(j * ms, 16), ms), :]

    def w_copy(k):
        return remote(w_rows(bas), w_rows(bas), w_ssem.at[k], w_rsem.at[k], at_x(k))

    def ws_copy(k):
        j = lax.rem(x + k, xn) * 2 + c
        return remote(w_rows(j), w_rows(j), ws_ssem.at[k], ws_rsem.at[k], sib)

    for k in range(1, xn):
        w_copy(k).start()
    ws_copy(0).start()

    def half_step(t, carry):
        b, g = t // GROUPS, lax.rem(t, GROUPS)
        acc = jnp.zeros((bs, gcol), F32)
        for s in range(0, nz, 2):
            lhs = jnp.concatenate([ints[b, s], ints[b, s + 1]], axis=1)
            rhs = jnp.concatenate([block_of(g, tab_smem[b, s]), block_of(g, tab_smem[b, s + 1])], axis=0)
            acc = acc + jnp.dot(lhs, rhs, preferred_element_type=F32)
        half[g, pl.ds(pl.multiple_of(b * bs, bs), bs), :] = acc.astype(BF16)
        return carry

    half_total = nrow * GROUPS
    lax.fori_loop(0, half_total // 2, half_step, 0)
    for k in range(1, xn):
        w_copy(k).wait()
        ws_copy(xn - k).start()
    lax.fori_loop(half_total // 2, half_total, half_step, 0)
    for k in range(xn):
        ws_copy(k).wait()

    tn = 256 if ncol % 256 == 0 else 128

    def exch_step(t, carry):
        n0 = pl.multiple_of(t * tn, tn)
        acc = jnp.zeros((krows, tn), F32)
        for g in range(GROUPS):
            acc = acc + lax.dot_general(
                wfull[g], half[g, pl.ds(n0, tn), :], (((1,), (1,)), ((), ())), preferred_element_type=F32)
        exch[:, pl.ds(n0, tn)] = acc
        return carry

    lax.fori_loop(0, ncol // tn, exch_step, 0)

    chunk_a, chunk_b = zn * out_rows, yn * out_rows
    per_z = yn * out_rows

    for t in range(yn):
        rows = jnp.concatenate(
            [exch[zz * per_z + t * out_rows : zz * per_z + (t + 1) * out_rows, :hcol] for zz in range(zn)], axis=0)
        send_a[t] = rows.astype(BF16)
    for t in range(zn):
        send_b[t] = exch[t * per_z : (t + 1) * per_z, hcol:].astype(BF16)

    def rs_a(k):
        to = lax.rem(y + k, yn)
        return remote(send_a.at[to], recv_a.at[y], rs_ssem.at[0, k], rs_rsem.at[0, k], at_y(k))

    def rs_b(k):
        to = lax.rem(z + k, zn)
        return remote(send_b.at[to], recv_b.at[z], rs_ssem.at[1, k], rs_rsem.at[1, k], at_z(k))

    for k in range(1, max(yn, zn)):
        if k < yn:
            rs_a(k).start()
        if k < zn:
            rs_b(k).start()
    recv_a[y] = send_a[y]
    recv_b[z] = send_b[z]

    def total(ref, n):
        acc = ref[0].astype(F32)
        for i in range(1, n):
            acc = acc + ref[i].astype(F32)
        return acc

    for k in range(1, yn):
        rs_a(k).wait()
    sum_a = total(recv_a, yn)
    for t in range(zn):
        send_a2[t] = sum_a[t * out_rows : (t + 1) * out_rows, :]

    def rs_a2(k):
        to = lax.rem(z + k, zn)
        return remote(send_a2.at[to], recv_a2.at[z], rs_ssem.at[2, k], rs_rsem.at[2, k], at_z(k))

    for k in range(1, zn):
        rs_a2(k).start()
    recv_a2[z] = send_a2[z]

    for k in range(1, zn):
        rs_b(k).wait()
    sum_b = total(recv_b, zn)
    for t in range(yn):
        send_b2[t] = sum_b[t * out_rows : (t + 1) * out_rows, :]

    def rs_b2(k):
        to = lax.rem(y + k, yn)
        return remote(send_b2.at[to], recv_b2.at[y], rs_ssem.at[3, k], rs_rsem.at[3, k], at_y(k))

    for k in range(1, yn):
        rs_b2(k).start()
    recv_b2[y] = send_b2[y]

    @pl.when(bas == 0)
    def _():
        for j in range(1, bas_n):
            remote(tab_vmem, tab_land, scat_ssem.at[j, 1], scat_rsem.at[1], (aux, j)).wait_send()
            remote(win_src(j), win, scat_ssem.at[j, 0], scat_rsem.at[0], (aux, j)).wait_send()

    def drain(s, carry):
        for st, q in every:
            ring_copy(st, q, s).wait_send()
            sib_copy(st, q, s).wait_send()
        return carry

    lax.fori_loop(0, steps, drain, 0)
    for st, q in every:
        sib_copy(st, q, steps).wait_send()
    for k in range(1, max(zn, yn)):
        if k < zn:
            ph2_copy(0, k).wait_send()
        if k < yn:
            ph2_copy(1, k).wait_send()

    factor = 1.0 / math.sqrt(aux_n * occ)
    for k in range(1, zn):
        rs_a2(k).wait()
    out_ref[:, :hcol] = total(recv_a2, zn) * factor
    for k in range(1, yn):
        rs_b2(k).wait()
    out_ref[:, hcol:] = total(recv_b2, yn) * factor


def on_device(dims, integrals, coefficients, metric, pair_blocks, pair_live):
    zn, yn, xn, bs, nz, nrow, occ, krows, rows_dev, nb = dims
    bas_n, aux_n = 2 * xn, zn * yn
    block = rows_dev * bas_n
    gcol = occ // GROUPS
    ms = krows // bas_n
    out_rows = krows // aux_n
    ncol = nrow * bs
    hcol = ncol // 2
    pad = -(-rows_dev // 16) * 16
    table = jnp.where(pair_live > 0, pair_blocks, nb // bs).astype(jnp.int32)
    table = jnp.pad(table, ((0, 8 - nrow), (0, 128 - nz)))
    v, dma = pltpu.VMEM, pltpu.SemaphoreType.DMA
    most = max(yn, zn)
    steps = yn - 1
    return pl.pallas_call(
        functools.partial(kernel, dims),
        out_shape=jax.ShapeDtypeStruct((out_rows, ncol), F32),
        in_specs=[
            pl.BlockSpec(memory_space=pl.ANY),
            pl.BlockSpec(memory_space=pltpu.VMEM),
            pl.BlockSpec(memory_space=pltpu.VMEM),
            pl.BlockSpec(memory_space=pltpu.SMEM),
            pl.BlockSpec(memory_space=pltpu.VMEM),
        ],
        out_specs=pl.BlockSpec(memory_space=pltpu.VMEM),
        scratch_shapes=[
            v((nrow, nz, bs, bs), BF16),
            v((pad, occ), F32),
            v((2, pad, occ // 2), BF16),
            v((bas_n, pad, occ // 2), BF16),
            v((block, occ // 2), F32),
            v((GROUPS, (nb + bs) // GRAN, GRAN, gcol), BF16),
            v((aux_n * 16, aux_n * 16), BF16),
            v((nz, ms, bs), BF16),
            v((zn, yn, 16, bs), BF16),
            v((yn, zn, 16, bs), BF16),
            v((zn, yn, 16, bs), BF16),
            v((zn, yn, 16, bs), BF16),
            v((yn, zn, 16, bs), BF16),
            v((zn, yn, 16, bs), BF16),
            v((nz, ms, bs), BF16),
            v((8, 128), jnp.int32),
            pltpu.SMEM((8, 128), jnp.int32),
            v((GROUPS, krows, gcol), BF16),
            v((GROUPS, ncol, gcol), BF16),
            v((krows, ncol), F32),
            v((yn, zn * out_rows, hcol), BF16),
            v((yn, zn * out_rows, hcol), BF16),
            v((zn, yn * out_rows, hcol), BF16),
            v((zn, yn * out_rows, hcol), BF16),
            v((zn, out_rows, hcol), F32),
            v((zn, out_rows, hcol), F32),
            v((yn, out_rows, hcol), F32),
            v((yn, out_rows, hcol), F32),
            dma((4,)),
            dma((bas_n,)), dma((bas_n,)),
            dma((bas_n, 2)), dma((2,)),
            dma((2, most)), dma((2, most)),
            dma((2, most, steps)), dma((2, most, steps)),
            dma((2, most, steps + 1)), dma((2, most, steps + 1)),
            dma((2, 2, most)), dma((2, 2, most)),
            dma((xn,)), dma((xn,)),
            dma((xn,)), dma((xn,)),
            dma((4, most)), dma((4, most)),
        ],
        compiler_params=pltpu.CompilerParams(
            collective_id=0, has_side_effects=True, vmem_limit_bytes=52 * 1024 * 1024),
        cost_estimate=pl.CostEstimate(
            flops=2 * (nrow * nz * bs * bs * occ + krows * ncol * occ), bytes_accessed=4 * 1024 * 1024,
            transcendentals=0),
    )(integrals[0], coefficients, metric, table, table)


def solution(mesh, grid=(8, 8)):
    zn, yn = grid
    xn = mesh.shape["bas"] // 2

    def whole(integrals, coefficients, metric, pair_blocks, pair_live):
        bs, nz = integrals.shape[-1], integrals.shape[2]
        nb, occ = coefficients.shape
        nrow = integrals.shape[1] // (2 * xn)
        krows = 512 if nb == 6144 else 128
        dims = (zn, yn, xn, bs, nz, nrow, occ, krows, nb // mesh.size, nb)
        return jax.shard_map(
            functools.partial(on_device, dims),
            mesh=mesh,
            in_specs=(
                P("aux", "bas", None, None, None),
                P(("aux", "bas"), None),
                P(),
                P("bas", None),
                P("bas", None),
            ),
            out_specs=P("aux", "bas"),
            check_vma=False,
        )(integrals, coefficients, metric, pair_blocks, pair_live)

    return whole
```

```python
import functools
import math

import jax
import jax.numpy as jnp
from jax import lax
from jax.experimental import pallas as pl
from jax.experimental.pallas import tpu as pltpu
from jax.sharding import PartitionSpec as P

BF16 = jnp.bfloat16
F32 = jnp.float32
GROUPS = 4
UNITS = 8
GRAN = 16
COMMON, PARITY = 1, 0


def wrap(value, n):
    assert n & (n - 1) == 0
    return value & (n - 1)


def kernel(
    dims,
    ints_hbm,
    coef_hbm,
    metric_hbm,
    blocks_hbm,
    live_hbm,
    out_ref,
    ints,
    coef_ref,
    metric_ref,
    raw_f32,
    raw_send,
    raw_recv,
    join_f32,
    coeff,
    kron,
    win,
    win_tiles,
    mid_a,
    mixin,
    mixed,
    mid_b,
    imix_tiles,
    imix,
    land_blocks,
    land_live,
    win_blocks,
    win_live,
    own_blocks,
    own_live,
    tab_z,
    tab_o,
    wfull,
    half,
    exch,
    send_a,
    recv_a,
    send_b,
    recv_b,
    send_a2,
    recv_a2,
    send_b2,
    recv_b2,
    local_sem,
    raw_ssem,
    raw_rsem,
    scat_ssem,
    scat_rsem,
    ph2_ssem,
    ph2_rsem,
    ring_ssem,
    ring_rsem,
    sib_ssem,
    sib_rsem,
    x_ssem,
    x_rsem,
    xsib_ssem,
    xsib_rsem,
    a2a_ssem,
    a2a_rsem,
    w_ssem,
    w_rsem,
    ws_ssem,
    ws_rsem,
    rs_ssem,
    rs_rsem,
):
    zn, yn, xn, bs, nz, nrow, occ, krows, rows_dev, nb = dims
    bas_n = 2 * xn
    aux_n = zn * yn
    block = rows_dev * bas_n
    gcol = occ // GROUPS
    ucol = occ // UNITS
    per = block // GRAN
    zh, yh = zn // 2, yn // 2
    ms = krows // bas_n
    out_rows = krows // aux_n
    ncol = nrow * bs
    hcol = ncol // 2
    dead = nb // bs

    aux = lax.axis_index("aux")
    bas = lax.axis_index("bas")
    y = wrap(aux, yn)
    z = (aux - y) // yn
    c = wrap(bas, 2)
    x = (bas - c) // 2
    par = wrap(x, 2)
    sib = (aux, x * 2 + 1 - c)

    def at_y(k):
        return (z * yn + wrap(y + k, yn), bas)

    def at_z(k):
        return (wrap(z + k, zn) * yn + y, bas)

    def at_bas(k):
        return (aux, wrap(bas + k, bas_n))

    def at_x(k):
        return (aux, wrap(x + k, xn) * 2 + c)

    def remote(src, dst, ssem, rsem, dev):
        return pltpu.make_async_remote_copy(
            src_ref=src, dst_ref=dst, send_sem=ssem, recv_sem=rsem,
            device_id=dev, device_id_type=pl.DeviceIdType.MESH)

    barrier = pltpu.get_barrier_semaphore()
    for k in range(1, yn):
        pl.semaphore_signal(barrier, inc=1, device_id=at_y(k), device_id_type=pl.DeviceIdType.MESH)
    for k in range(1, zn):
        pl.semaphore_signal(barrier, inc=1, device_id=at_z(k), device_id_type=pl.DeviceIdType.MESH)
    for k in range(1, bas_n):
        pl.semaphore_signal(barrier, inc=1, device_id=at_bas(k), device_id_type=pl.DeviceIdType.MESH)

    fetch_coef = pltpu.make_async_copy(coef_hbm, coef_ref, local_sem.at[6])
    fetch_coef.start()
    fetch_metric = pltpu.make_async_copy(metric_hbm, metric_ref, local_sem.at[7])
    fetch_metric.start()
    fetch = pltpu.make_async_copy(ints_hbm, ints, local_sem.at[0])
    fetch.start()
    own_tabs = [
        pltpu.make_async_copy(blocks_hbm, own_blocks, local_sem.at[3]),
        pltpu.make_async_copy(live_hbm, own_live, local_sem.at[4]),
    ]
    for copy in own_tabs:
        copy.start()
    raw_f32[...] = jnp.zeros_like(raw_f32)
    fetch_coef.wait()
    raw_f32[0:rows_dev, :] = coef_ref[...].astype(F32)
    packed = raw_f32[...].astype(BF16)
    raw_send[0] = packed[:, : occ // 2]
    raw_send[1] = packed[:, occ // 2 :]
    pl.semaphore_wait(barrier, yn - 1 + zn - 1 + bas_n - 1)

    def raw_copy(k):
        to = wrap(bas + k, bas_n)
        return remote(raw_send.at[wrap(to, 2)], raw_recv.at[bas], raw_ssem.at[k], raw_rsem.at[k], (aux, to))

    for k in range(1, bas_n):
        raw_copy(k).start()
    raw_recv[bas] = raw_send[c]

    def win_src(j):
        b = (j * ms) // bs
        off = (j * ms) % bs
        return ints_hbm.at[b, :, pl.ds(off, ms), :]

    def scatter(j):
        return [
            remote(blocks_hbm, land_blocks, scat_ssem.at[j, 1], scat_rsem.at[1], (aux, j)),
            remote(live_hbm, land_live, scat_ssem.at[j, 2], scat_rsem.at[2], (aux, j)),
            remote(win_src(j), win, scat_ssem.at[j, 0], scat_rsem.at[0], (aux, j)),
        ]

    @pl.when(bas == 0)
    def _():
        for j in range(1, bas_n):
            for copy in scatter(j):
                copy.start()
        pltpu.make_async_copy(blocks_hbm, land_blocks, local_sem.at[2]).start()
        pltpu.make_async_copy(live_hbm, land_live, local_sem.at[5]).start()
        pltpu.make_async_copy(win_src(0), win, local_sem.at[1]).start()

    for k in range(1, bas_n):
        raw_copy(k).wait()
    for j in range(bas_n):
        join_f32[j * rows_dev : (j + 1) * rows_dev, :] = raw_recv[j][0:rows_dev, :].astype(F32)

    def unit(st, kind):
        return 4 * c + st if kind == COMMON else 4 * c + 2 + par

    joined = join_f32[...].astype(BF16)
    cols = [joined[:, k * ucol : (k + 1) * ucol].reshape(per, GRAN, ucol) for k in range(4)]
    for st in range(2):
        coeff[unit(st, COMMON), z, pl.ds(y * per, per)] = cols[st]
    coeff[unit(0, PARITY), z, pl.ds(y * per, per)] = jnp.where(par == 0, cols[2], cols[3])

    def both(kind, run):
        if kind == COMMON:
            run(0)
            run(1)
        else:
            pl.when(c == 0)(lambda: run(0))
            pl.when(c == 1)(lambda: run(1))

    def ph2_copy(st, kind, k):
        ref = coeff.at[unit(st, kind), z, pl.ds(y * per, per)]
        return remote(
            ref, ref, ph2_ssem.at[st, kind, k], ph2_rsem.at[st, kind, k], at_z(k) if st == 0 else at_y(k))

    def near_first(n):
        return sorted(range(1, n), key=lambda k: min(k, n - k))

    def ph2_start(kind):
        def run(st):
            for k in near_first(zn if st == 0 else yn):
                ph2_copy(st, kind, k).start()
        both(kind, run)

    def ph2_drain(kind):
        def run(st):
            for k in range(1, zn if st == 0 else yn):
                ph2_copy(st, kind, k).wait_send()
        both(kind, run)

    ph2_start(PARITY)
    ph2_start(COMMON)

    def half_slab(u, st, d, h, s):
        n, me = (yn, y) if st == 0 else (zn, z)
        pos = wrap(me + (n - s if d == 0 else s), n)
        if st == 0:
            return coeff.at[u, pl.ds(h * zh, zh), pl.ds(pos * per, per)]
        return coeff.at[u, pos, pl.ds(h * yh * per, yh * per)]

    far = yn // 2

    def next_at(st, d):
        n, at = (yn, at_y) if st == 0 else (zn, at_z)
        return at(1) if d == 0 else at(n - 1)

    def ring_copy(st, kind, d, h, s):
        ref = half_slab(unit(st, kind), st, d, h, s)
        return remote(ref, ref, ring_ssem.at[st, kind, d], ring_rsem.at[st, kind, d, h, s], next_at(st, d))

    def ring_block(st, kind, q):
        zz, yy = (q, y) if st == 0 else (z, q)
        ref = coeff.at[unit(st, kind), zz, pl.ds(yy * per, per)]
        h = q // (zh if st == 0 else yh)
        for d in range(2):
            copy = remote(ref, ref, ring_ssem.at[st, kind, d], ring_rsem.at[st, kind, d, h, 0], next_at(st, d))
            if far > 1:
                copy.start()
            else:
                pl.when(h == d)(copy.start)

    def sib_copy(st, kind, d, h, s):
        ref = half_slab(unit(st, kind), st, d, h, s)
        return remote(ref, ref, sib_ssem.at[st, kind], sib_rsem.at[st, kind], sib)

    def x_copy(st, d, h, s):
        ref = half_slab(unit(st, PARITY), st, d, h, s)
        return remote(ref, ref, x_ssem.at[0], x_rsem.at[d, h, s], at_x(1) if h == 0 else at_x(xn - 1))

    def xsib_copy(st, d, h, s):
        ref = half_slab(4 * c + 3 - par, st, d, h, s)
        return remote(ref, ref, xsib_ssem.at[0], xsib_rsem.at[0], sib)

    def all_of(n, ssem, rsem):
        if n == 2 * zn:
            ref = coeff.at[0, pl.ds(0, zn)]
        else:
            ref = coeff.at[0, pl.ds(0, n), pl.ds(0, yh * per)]
        return remote(ref, ref, ssem, rsem, sib)

    def halves(s):
        if s == 0:
            return [(0, 0), (0, 1)]
        return [(d, h) for h in range(2) for d in range(2) if s < far or h == d]

    def own_slab():
        for kind in (PARITY, COMMON):
            both(kind, lambda st: ring_block(st, kind, z if st == 0 else y))
        for k in near_first(yn):
            for kind in (PARITY, COMMON):
                def run(st):
                    n, me = (zn, z) if st == 0 else (yn, y)
                    ph2_copy(st, kind, k).wait_recv()
                    ring_block(st, kind, wrap(me + n - k, n))
                both(kind, run)
        for kind in (PARITY, COMMON):
            arrive(kind, 0)

    def arrive(kind, s):
        def run(st):
            for d, h in halves(s):
                if s > 0:
                    ring_copy(st, kind, d, h, s - 1).wait_recv()
                    if s + 1 < far or (s + 1 == far and h == d):
                        ring_copy(st, kind, d, h, s).start()
                if kind == PARITY:
                    x_copy(st, d, h, s).start()
                sib_copy(st, kind, d, h, s).start()
        both(kind, run)

    def x_arrive(s):
        def run(st):
            for d, h in halves(s):
                x_copy(st, d, h, s).wait_recv()
                xsib_copy(st, d, h, s).start()
        both(PARITY, run)

    def sib_arrive(kind):
        def run(st):
            all_of(2 * zn, sib_ssem.at[st, kind], sib_rsem.at[st, kind]).wait_recv()
        if kind == COMMON:
            run(0)
            run(1)
        else:
            pl.when(c == 1)(lambda: run(0))
            pl.when(c == 0)(lambda: run(1))
            all_of(2 * zn, xsib_ssem.at[0], xsib_rsem.at[0]).wait_recv()

    def gather_drain(kind):
        def run(st):
            all_of(2 * zn, sib_ssem.at[st, kind], sib_rsem.at[st, kind]).wait_send()
            for d in range(2):
                all_of(yn - 1, ring_ssem.at[st, kind, d], ring_rsem.at[st, kind, d, 0, 0]).wait_send()
        if kind == PARITY:
            all_of(2 * zn, xsib_ssem.at[0], xsib_rsem.at[0]).wait_send()
            all_of(2 * zn, x_ssem.at[0], x_rsem.at[0, 0, 0]).wait_send()
        both(kind, run)
        ph2_drain(kind)

    krow = yn * 16

    def make_kron():
        fetch_metric.wait()
        metric = metric_ref[...]
        gram = lax.dot_general(metric, metric, (((0,), (0,)), ((), ())), preferred_element_type=F32).astype(BF16)
        spread_c = (
            lax.broadcasted_iota(jnp.int32, (aux_n, aux_n * 16), 0)
            == (lax.broadcasted_iota(jnp.int32, (aux_n, aux_n * 16), 1) >> 4)
        ).astype(F32).astype(BF16)

        def kron_step(t, carry):
            r0 = pl.multiple_of(t * krow, krow)
            spread_r = (
                ((lax.broadcasted_iota(jnp.int32, (krow, aux_n), 0) + r0) >> 4)
                == lax.broadcasted_iota(jnp.int32, (krow, aux_n), 1)
            ).astype(F32).astype(BF16)
            rows = jnp.dot(spread_r, gram, preferred_element_type=F32).astype(BF16)
            full = jnp.dot(rows, spread_c, preferred_element_type=F32)
            same = (lax.broadcasted_iota(jnp.int32, full.shape, 0) & 15) == (
                lax.broadcasted_iota(jnp.int32, full.shape, 1) & 15)
            kron[pl.ds(r0, krow), :] = jnp.where(same, full, 0.0).astype(BF16)
            return carry

        lax.fori_loop(0, aux_n * 16 // krow, kron_step, 0)
        for u in range(UNITS):
            coeff[u, zn, 0 : bs // GRAN] = jnp.zeros((bs // GRAN, GRAN, ucol), BF16)

    def a2a_y(i, src, mid, k):
        to = wrap(y + k, yn)
        return remote(src.at[:, to], mid.at[y], a2a_ssem.at[i, 0, k], a2a_rsem.at[i, 0, k], at_y(k))

    def a2a_z(i, mid, dst, k):
        to = wrap(z + k, zn)
        return remote(mid.at[:, to], dst.at[z], a2a_ssem.at[i, 1, k], a2a_rsem.at[i, 1, k], at_z(k))

    def a2a_y_start(i, src, mid):
        for k in range(1, yn):
            a2a_y(i, src, mid, k).start()
        mid[y] = src[:, y]

    def a2a_z_start(i, src, mid, dst):
        for k in range(1, yn):
            a2a_y(i, src, mid, k).wait()
        for k in range(1, zn):
            a2a_z(i, mid, dst, k).start()
        dst[z] = mid[:, z]

    def a2a_end(i, mid, dst):
        for k in range(1, zn):
            a2a_z(i, mid, dst, k).wait()

    def scatter_arrive():
        @pl.when(bas == 0)
        def _():
            pltpu.make_async_copy(blocks_hbm, land_blocks, local_sem.at[2]).wait()
            pltpu.make_async_copy(live_hbm, land_live, local_sem.at[5]).wait()
            pltpu.make_async_copy(win_src(0), win, local_sem.at[1]).wait()

        @pl.when(bas != 0)
        def _():
            for copy in scatter(0):
                copy.wait_recv()

        win_tiles[...] = win[...].reshape(zn, yn, 16, bs)

    per_z = yn * block // bs

    def tables():
        win_tabs = [
            pltpu.make_async_copy(land_blocks, win_blocks, local_sem.at[2]),
            pltpu.make_async_copy(land_live, win_live, local_sem.at[5]),
        ]
        for copy in win_tabs:
            copy.start()
        for copy in own_tabs + win_tabs:
            copy.wait()
        wrow = (bas * ms) // bs

        def fill(s, carry):
            for b in range(nrow + 1):
                if b < nrow:
                    blk, live = own_blocks[b, s], own_live[b, s]
                else:
                    blk, live = win_blocks[wrow, s], win_live[wrow, s]
                place = live * (blk - dead) + dead
                tab_z[b, s] = lax.div(place, per_z)
                tab_o[b, s] = lax.rem(place, per_z) * (bs // GRAN)
            return carry

        lax.fori_loop(0, nz, fill, 0)

    def mix():
        def mix_step(t, carry):
            r0 = pl.multiple_of(t * krow, krow)
            rows = jnp.dot(
                kron[pl.ds(r0, krow), :], mixin[...].reshape(aux_n * 16, bs), preferred_element_type=F32)
            mixed[t] = rows.astype(BF16).reshape(yn, 16, bs)
            return carry

        lax.fori_loop(0, zn, mix_step, 0)

    def chain(k):
        if k == CHAIN[0]:
            scatter_arrive()
            a2a_y_start(0, win_tiles, mid_a)
            make_kron()
        if k == CHAIN[1]:
            a2a_z_start(0, win_tiles, mid_a, mixin)
            tables()
        if k == CHAIN[2]:
            a2a_end(0, mid_a, mixin)
            mix()
            a2a_y_start(1, mixed, mid_b)
        if k == CHAIN[3]:
            a2a_z_start(1, mixed, mid_b, imix_tiles)

    CHAIN = [min(k, far) for k in (0, 1, 2, 3)]
    own_slab()
    chain(0)
    for k in range(1, far + 1):
        arrive(PARITY, k)
        arrive(COMMON, k)
        x_arrive(k - 1)
        chain(k)
    x_arrive(far)
    a2a_end(1, mid_b, imix_tiles)
    imix[...] = imix_tiles[...].reshape(nz, ms, bs)
    fetch.wait()
    sib_arrive(PARITY)
    sib_arrive(COMMON)

    def block_of(g, b, s):
        zi, off = tab_z[b, s], tab_o[b, s]
        return jnp.concatenate(
            [coeff[2 * g + i, zi, pl.ds(off, bs // GRAN)].reshape(bs, ucol) for i in range(2)], axis=1)

    def w_step(g, carry):
        acc = jnp.zeros((ms, gcol), F32)
        for s in range(0, nz, 2):
            lhs = jnp.concatenate([imix[s], imix[s + 1]], axis=1)
            rhs = jnp.concatenate([block_of(g, nrow, s), block_of(g, nrow, s + 1)], axis=0)
            acc = acc + jnp.dot(lhs, rhs, preferred_element_type=F32)
        wfull[g, pl.ds(pl.multiple_of(bas * ms, 16), ms), :] = acc.astype(BF16)
        return carry

    lax.fori_loop(0, GROUPS, w_step, 0)

    def w_rows(j):
        return wfull.at[:, pl.ds(pl.multiple_of(j * ms, 16), ms), :]

    def w_copy(k):
        return remote(w_rows(bas), w_rows(bas), w_ssem.at[k], w_rsem.at[k], at_x(k))

    def ws_copy(k):
        j = wrap(x + k, xn) * 2 + c
        return remote(w_rows(j), w_rows(j), ws_ssem.at[k], ws_rsem.at[k], sib)

    for k in range(1, xn):
        w_copy(k).start()
    ws_copy(0).start()

    def half_step(t, carry):
        b, g = t // GROUPS, lax.rem(t, GROUPS)
        acc = jnp.zeros((bs, gcol), F32)
        for s in range(0, nz, 2):
            lhs = jnp.concatenate([ints[b, s], ints[b, s + 1]], axis=1)
            rhs = jnp.concatenate([block_of(g, b, s), block_of(g, b, s + 1)], axis=0)
            acc = acc + jnp.dot(lhs, rhs, preferred_element_type=F32)
        half[g, pl.ds(pl.multiple_of(b * bs, bs), bs), :] = acc.astype(BF16)
        return carry

    half_total = nrow * GROUPS
    lax.fori_loop(0, half_total // 2, half_step, 0)
    for k in range(1, xn):
        w_copy(k).wait()
        ws_copy(xn - k).start()
    lax.fori_loop(half_total // 2, half_total, half_step, 0)
    for k in range(xn):
        ws_copy(k).wait()

    tn = 256 if ncol % 256 == 0 else 128

    def exch_step(t, carry):
        n0 = pl.multiple_of(t * tn, tn)
        acc = jnp.zeros((krows, tn), F32)
        for g in range(GROUPS):
            acc = acc + lax.dot_general(
                wfull[g], half[g, pl.ds(n0, tn), :], (((1,), (1,)), ((), ())), preferred_element_type=F32)
        exch[:, pl.ds(n0, tn)] = acc
        return carry

    lax.fori_loop(0, ncol // tn, exch_step, 0)

    zrows = yn * out_rows

    for t in range(yn):
        rows = jnp.concatenate(
            [exch[zz * zrows + t * out_rows : zz * zrows + (t + 1) * out_rows, :hcol] for zz in range(zn)], axis=0)
        send_a[t] = rows.astype(BF16)
    for t in range(zn):
        send_b[t] = exch[t * zrows : (t + 1) * zrows, hcol:].astype(BF16)

    def rs_a(k):
        to = wrap(y + k, yn)
        return remote(send_a.at[to], recv_a.at[y], rs_ssem.at[0, k], rs_rsem.at[0, k], at_y(k))

    def rs_b(k):
        to = wrap(z + k, zn)
        return remote(send_b.at[to], recv_b.at[z], rs_ssem.at[1, k], rs_rsem.at[1, k], at_z(k))

    for k in range(1, max(yn, zn)):
        if k < yn:
            rs_a(k).start()
        if k < zn:
            rs_b(k).start()
    recv_a[y] = send_a[y]
    recv_b[z] = send_b[z]

    @pl.when(bas == 0)
    def _():
        for j in range(1, bas_n):
            for copy in scatter(j):
                copy.wait_send()

    gather_drain(PARITY)
    gather_drain(COMMON)

    def total(ref, n):
        acc = ref[0].astype(F32)
        for i in range(1, n):
            acc = acc + ref[i].astype(F32)
        return acc

    for k in range(1, yn):
        rs_a(k).wait()
    sum_a = total(recv_a, yn)
    for t in range(zn):
        send_a2[t] = sum_a[t * out_rows : (t + 1) * out_rows, :]

    def rs_a2(k):
        to = wrap(z + k, zn)
        return remote(send_a2.at[to], recv_a2.at[z], rs_ssem.at[2, k], rs_rsem.at[2, k], at_z(k))

    for k in range(1, zn):
        rs_a2(k).start()
    recv_a2[z] = send_a2[z]

    for k in range(1, zn):
        rs_b(k).wait()
    sum_b = total(recv_b, zn)
    for t in range(yn):
        send_b2[t] = sum_b[t * out_rows : (t + 1) * out_rows, :]

    def rs_b2(k):
        to = wrap(y + k, yn)
        return remote(send_b2.at[to], recv_b2.at[y], rs_ssem.at[3, k], rs_rsem.at[3, k], at_y(k))

    for k in range(1, yn):
        rs_b2(k).start()
    recv_b2[y] = send_b2[y]

    factor = 1.0 / math.sqrt(aux_n * occ)
    for k in range(1, zn):
        rs_a2(k).wait()
    out_ref[:, :hcol] = total(recv_a2, zn) * factor
    for k in range(1, yn):
        rs_b2(k).wait()
    out_ref[:, hcol:] = total(recv_b2, yn) * factor


def on_device(dims, integrals, coefficients, metric, pair_blocks, pair_live):
    zn, yn, xn, bs, nz, nrow, occ, krows, rows_dev, nb = dims
    bas_n, aux_n = 2 * xn, zn * yn
    block = rows_dev * bas_n
    gcol = occ // GROUPS
    ms = krows // bas_n
    out_rows = krows // aux_n
    ncol = nrow * bs
    hcol = ncol // 2
    pad = -(-rows_dev // 16) * 16
    v, dma = pltpu.VMEM, pltpu.SemaphoreType.DMA
    most = max(yn, zn)
    return pl.pallas_call(
        functools.partial(kernel, dims),
        out_shape=jax.ShapeDtypeStruct((out_rows, ncol), F32),
        in_specs=[pl.BlockSpec(memory_space=pltpu.HBM)] * 5,
        out_specs=pl.BlockSpec(memory_space=pltpu.VMEM),
        scratch_shapes=[
            v((nrow, nz, bs, bs), BF16),
            v((rows_dev, occ), BF16),
            v((aux_n, aux_n), BF16),
            v((pad, occ), F32),
            v((2, pad, occ // 2), BF16),
            v((bas_n, pad, occ // 2), BF16),
            v((block, occ // 2), F32),
            v((UNITS, zn + 1, yn * block // GRAN, GRAN, occ // UNITS), BF16),
            v((aux_n * 16, aux_n * 16), BF16),
            v((nz, ms, bs), BF16),
            v((zn, yn, 16, bs), BF16),
            v((yn, zn, 16, bs), BF16),
            v((zn, yn, 16, bs), BF16),
            v((zn, yn, 16, bs), BF16),
            v((yn, zn, 16, bs), BF16),
            v((zn, yn, 16, bs), BF16),
            v((nz, ms, bs), BF16),
            v((nrow, nz), jnp.int32),
            v((nrow, nz), jnp.int32),
            pltpu.SMEM((nrow, nz), jnp.int32),
            pltpu.SMEM((nrow, nz), jnp.int32),
            pltpu.SMEM((nrow, nz), jnp.int32),
            pltpu.SMEM((nrow, nz), jnp.int32),
            pltpu.SMEM((nrow + 1, nz), jnp.int32),
            pltpu.SMEM((nrow + 1, nz), jnp.int32),
            v((GROUPS, krows, gcol), BF16),
            v((GROUPS, ncol, gcol), BF16),
            v((krows, ncol), F32),
            v((yn, zn * out_rows, hcol), BF16),
            v((yn, zn * out_rows, hcol), BF16),
            v((zn, yn * out_rows, hcol), BF16),
            v((zn, yn * out_rows, hcol), BF16),
            v((zn, out_rows, hcol), F32),
            v((zn, out_rows, hcol), F32),
            v((yn, out_rows, hcol), F32),
            v((yn, out_rows, hcol), F32),
            dma((8,)),
            dma((bas_n,)), dma((bas_n,)),
            dma((bas_n, 3)), dma((3,)),
            dma((2, 2, most)), dma((2, 2, most)),
            dma((2, 2, 2)), dma((2, 2, 2, 2, most)),
            dma((2, 2)), dma((2, 2)),
            dma((1,)), dma((2, 2, most)),
            dma((1,)), dma((1,)),
            dma((2, 2, most)), dma((2, 2, most)),
            dma((xn,)), dma((xn,)),
            dma((xn,)), dma((xn,)),
            dma((4, most)), dma((4, most)),
        ],
        compiler_params=pltpu.CompilerParams(
            collective_id=0, has_side_effects=True, vmem_limit_bytes=52 * 1024 * 1024),
        cost_estimate=pl.CostEstimate(
            flops=2 * (nrow * nz * bs * bs * occ + krows * ncol * occ), bytes_accessed=4 * 1024 * 1024,
            transcendentals=0),
    )(integrals[0], coefficients, metric, pair_blocks, pair_live)


def solution(mesh, grid=(8, 8)):
    zn, yn = grid
    xn = mesh.shape["bas"] // 2

    def whole(integrals, coefficients, metric, pair_blocks, pair_live):
        bs, nz = integrals.shape[-1], integrals.shape[2]
        nb, occ = coefficients.shape
        nrow = integrals.shape[1] // (2 * xn)
        krows = 512 if nb == 6144 else 128
        dims = (zn, yn, xn, bs, nz, nrow, occ, krows, nb // mesh.size, nb)
        return jax.shard_map(
            functools.partial(on_device, dims),
            mesh=mesh,
            in_specs=(
                P("aux", "bas", None, None, None),
                P(("aux", "bas"), None),
                P(),
                P("bas", None),
                P("bas", None),
            ),
            out_specs=P("aux", "bas"),
            check_vma=False,
        )(integrals, coefficients, metric, pair_blocks, pair_live)

    return whole
```

```python
import functools
import math

import jax
import jax.numpy as jnp
from jax import lax
from jax.experimental import pallas as pl
from jax.experimental.pallas import tpu as pltpu
from jax.sharding import PartitionSpec as P

BF16 = jnp.bfloat16
F32 = jnp.float32
GROUPS = 4
UNITS = 8
GRAN = 16
COMMON, PARITY = 1, 0


def wrap(value, n):
    assert n & (n - 1) == 0
    return value & (n - 1)


def far_first(n):
    return sorted(range(1, n), key=lambda k: -min(k, n - k))


def kernel(
    dims,
    ints_hbm,
    coef_hbm,
    metric_hbm,
    blocks_hbm,
    live_hbm,
    out_ref,
    ints,
    coef_ref,
    metric_ref,
    raw_f32,
    raw_send,
    raw_recv,
    join_f32,
    coeff,
    kron,
    win,
    win_tiles,
    mid_a,
    mixin,
    mixed,
    mid_b,
    imix_tiles,
    imix,
    land_blocks,
    land_live,
    win_blocks,
    win_live,
    own_blocks,
    own_live,
    tab_z,
    tab_o,
    wfull,
    half,
    exch,
    send_a,
    recv_a,
    send_b,
    recv_b,
    send_a2,
    recv_a2,
    send_b2,
    recv_b2,
    local_sem,
    raw_ssem,
    raw_rsem,
    scat_ssem,
    scat_rsem,
    ph2_ssem,
    ph2_rsem,
    ring_ssem,
    ring_rsem,
    sib_ssem,
    sib_rsem,
    x_ssem,
    x_rsem,
    xsib_ssem,
    xsib_rsem,
    a2a_ssem,
    a2a_rsem,
    w_ssem,
    w_rsem,
    ws_ssem,
    ws_rsem,
    rs_ssem,
    rs_rsem,
    rsb_ssem,
    rsb_rsem,
):
    zn, yn, xn, bs, nz, nrow, occ, krows, rows_dev, nb = dims
    bas_n = 2 * xn
    aux_n = zn * yn
    block = rows_dev * bas_n
    gcol = occ // GROUPS
    ucol = occ // UNITS
    per = block // GRAN
    zh, yh = zn // 2, yn // 2
    ms = krows // bas_n
    out_rows = krows // aux_n
    mh = ms // 2
    assert ms == yn * out_rows
    ncol = nrow * bs
    hcol = ncol // 2
    dead = nb // bs

    aux = lax.axis_index("aux")
    bas = lax.axis_index("bas")
    y = wrap(aux, yn)
    z = (aux - y) // yn
    c = wrap(bas, 2)
    x = (bas - c) // 2
    par = wrap(x, 2)
    sib = (aux, x * 2 + 1 - c)

    def at_y(k):
        return (z * yn + wrap(y + k, yn), bas)

    def at_z(k):
        return (wrap(z + k, zn) * yn + y, bas)

    def at_bas(k):
        return (aux, wrap(bas + k, bas_n))

    def at_x(k):
        return (aux, wrap(x + k, xn) * 2 + c)

    def remote(src, dst, ssem, rsem, dev):
        return pltpu.make_async_remote_copy(
            src_ref=src, dst_ref=dst, send_sem=ssem, recv_sem=rsem,
            device_id=dev, device_id_type=pl.DeviceIdType.MESH)

    barrier = pltpu.get_barrier_semaphore()
    for k in range(1, yn):
        pl.semaphore_signal(barrier, inc=1, device_id=at_y(k), device_id_type=pl.DeviceIdType.MESH)
    for k in range(1, zn):
        pl.semaphore_signal(barrier, inc=1, device_id=at_z(k), device_id_type=pl.DeviceIdType.MESH)
    for k in range(1, bas_n):
        pl.semaphore_signal(barrier, inc=1, device_id=at_bas(k), device_id_type=pl.DeviceIdType.MESH)

    fetch_coef = pltpu.make_async_copy(coef_hbm, coef_ref, local_sem.at[6])
    fetch_coef.start()
    fetch_metric = pltpu.make_async_copy(metric_hbm, metric_ref, local_sem.at[7])
    fetch_metric.start()
    fetch = pltpu.make_async_copy(ints_hbm, ints, local_sem.at[0])
    fetch.start()
    own_tabs = [
        pltpu.make_async_copy(blocks_hbm, own_blocks, local_sem.at[3]),
        pltpu.make_async_copy(live_hbm, own_live, local_sem.at[4]),
    ]
    for copy in own_tabs:
        copy.start()
    raw_f32[...] = jnp.zeros_like(raw_f32)
    fetch_coef.wait()
    raw_f32[0:rows_dev, :] = coef_ref[...].astype(F32)
    packed = raw_f32[...].astype(BF16)
    raw_send[0] = packed[:, : occ // 2]
    raw_send[1] = packed[:, occ // 2 :]
    pl.semaphore_wait(barrier, yn - 1 + zn - 1 + bas_n - 1)

    def raw_copy(k):
        to = wrap(bas + k, bas_n)
        return remote(raw_send.at[wrap(to, 2)], raw_recv.at[bas], raw_ssem.at[k], raw_rsem.at[k], (aux, to))

    for k in far_first(bas_n):
        raw_copy(k).start()
    raw_recv[bas] = raw_send[c]

    def win_src(j):
        b = (j * ms) // bs
        off = (j * ms) % bs
        return ints_hbm.at[b, :, pl.ds(off, ms), :]

    def scatter(j):
        return [
            remote(blocks_hbm, land_blocks, scat_ssem.at[j, 1], scat_rsem.at[1], (aux, j)),
            remote(live_hbm, land_live, scat_ssem.at[j, 2], scat_rsem.at[2], (aux, j)),
            remote(win_src(j), win, scat_ssem.at[j, 0], scat_rsem.at[0], (aux, j)),
        ]

    @pl.when(bas == 0)
    def _():
        for j in range(1, bas_n):
            for copy in scatter(j):
                copy.start()
        pltpu.make_async_copy(blocks_hbm, land_blocks, local_sem.at[2]).start()
        pltpu.make_async_copy(live_hbm, land_live, local_sem.at[5]).start()
        pltpu.make_async_copy(win_src(0), win, local_sem.at[1]).start()

    for k in range(1, bas_n):
        raw_copy(k).wait()
    for j in range(bas_n):
        join_f32[j * rows_dev : (j + 1) * rows_dev, :] = raw_recv[j][0:rows_dev, :].astype(F32)

    def unit(st, kind):
        return 4 * c + st if kind == COMMON else 4 * c + 2 + par

    joined = join_f32[...].astype(BF16)
    cols = [joined[:, k * ucol : (k + 1) * ucol].reshape(per, GRAN, ucol) for k in range(4)]
    for st in range(2):
        coeff[unit(st, COMMON), z, pl.ds(y * per, per)] = cols[st]
    coeff[unit(0, PARITY), z, pl.ds(y * per, per)] = jnp.where(par == 0, cols[2], cols[3])

    def both(kind, run):
        if kind == COMMON:
            run(0)
            run(1)
        else:
            pl.when(c == 0)(lambda: run(0))
            pl.when(c == 1)(lambda: run(1))

    def ph2_copy(st, kind, k):
        ref = coeff.at[unit(st, kind), z, pl.ds(y * per, per)]
        return remote(
            ref, ref, ph2_ssem.at[st, kind, k], ph2_rsem.at[st, kind, k], at_z(k) if st == 0 else at_y(k))

    def near_first(n):
        return sorted(range(1, n), key=lambda k: min(k, n - k))

    def ph2_start(kind):
        def run(st):
            for k in near_first(zn if st == 0 else yn):
                ph2_copy(st, kind, k).start()
        both(kind, run)

    def ph2_drain(kind):
        def run(st):
            for k in range(1, zn if st == 0 else yn):
                ph2_copy(st, kind, k).wait_send()
        both(kind, run)

    ph2_start(COMMON)
    ph2_start(PARITY)

    def half_slab(u, st, d, h, s):
        n, me = (yn, y) if st == 0 else (zn, z)
        pos = wrap(me + (n - s if d == 0 else s), n)
        if st == 0:
            return coeff.at[u, pl.ds(h * zh, zh), pl.ds(pos * per, per)]
        return coeff.at[u, pos, pl.ds(h * yh * per, yh * per)]

    far = yn // 2

    def next_at(st, d):
        n, at = (yn, at_y) if st == 0 else (zn, at_z)
        return at(1) if d == 0 else at(n - 1)

    def ring_copy(st, kind, d, h, s):
        ref = half_slab(unit(st, kind), st, d, h, s)
        return remote(ref, ref, ring_ssem.at[st, kind, d], ring_rsem.at[st, kind, d, h, s], next_at(st, d))

    def ring_block(st, kind, q):
        zz, yy = (q, y) if st == 0 else (z, q)
        ref = coeff.at[unit(st, kind), zz, pl.ds(yy * per, per)]
        h = q // (zh if st == 0 else yh)
        for d in range(2):
            copy = remote(ref, ref, ring_ssem.at[st, kind, d], ring_rsem.at[st, kind, d, h, 0], next_at(st, d))
            if far > 1:
                copy.start()
            else:
                pl.when(h == d)(copy.start)

    def sib_copy(st, kind, d, h, s):
        ref = half_slab(unit(st, kind), st, d, h, s)
        return remote(ref, ref, sib_ssem.at[st, kind], sib_rsem.at[st, kind], sib)

    def x_copy(st, d, h, s):
        ref = half_slab(unit(st, PARITY), st, d, h, s)
        return remote(ref, ref, x_ssem.at[0], x_rsem.at[d, h, s], at_x(1) if h == 0 else at_x(xn - 1))

    def xsib_copy(st, d, h, s):
        ref = half_slab(4 * c + 3 - par, st, d, h, s)
        return remote(ref, ref, xsib_ssem.at[0], xsib_rsem.at[0], sib)

    def all_of(n, ssem, rsem):
        if n == 2 * zn:
            ref = coeff.at[0, pl.ds(0, zn)]
        else:
            ref = coeff.at[0, pl.ds(0, n), pl.ds(0, yh * per)]
        return remote(ref, ref, ssem, rsem, sib)

    def halves(s):
        if s == 0:
            return [(0, 0), (0, 1)]
        return [(d, h) for h in range(2) for d in range(2) if s < far or h == d]

    def own_slab():
        for kind in (COMMON, PARITY):
            both(kind, lambda st: ring_block(st, kind, z if st == 0 else y))
        for k in near_first(yn):
            for kind in (COMMON, PARITY):
                def run(st):
                    n, me = (zn, z) if st == 0 else (yn, y)
                    ph2_copy(st, kind, k).wait_recv()
                    ring_block(st, kind, wrap(me + n - k, n))
                both(kind, run)
        for kind in (COMMON, PARITY):
            arrive(kind, 0)

    def arrive(kind, s):
        def run(st):
            for d, h in halves(s):
                if s > 0:
                    ring_copy(st, kind, d, h, s - 1).wait_recv()
                    if s + 1 < far or (s + 1 == far and h == d):
                        ring_copy(st, kind, d, h, s).start()
                if kind == PARITY:
                    x_copy(st, d, h, s).start()
                sib_copy(st, kind, d, h, s).start()
        both(kind, run)

    def x_arrive(s):
        def run(st):
            for d, h in halves(s):
                x_copy(st, d, h, s).wait_recv()
                xsib_copy(st, d, h, s).start()
        both(PARITY, run)

    def sib_arrive(kind):
        def run(st):
            all_of(2 * zn, sib_ssem.at[st, kind], sib_rsem.at[st, kind]).wait_recv()
        if kind == COMMON:
            run(0)
            run(1)
        else:
            pl.when(c == 1)(lambda: run(0))
            pl.when(c == 0)(lambda: run(1))
            all_of(2 * zn, xsib_ssem.at[0], xsib_rsem.at[0]).wait_recv()

    def gather_drain(kind):
        def run(st):
            all_of(2 * zn, sib_ssem.at[st, kind], sib_rsem.at[st, kind]).wait_send()
            for d in range(2):
                all_of(yn - 1, ring_ssem.at[st, kind, d], ring_rsem.at[st, kind, d, 0, 0]).wait_send()
        if kind == PARITY:
            all_of(2 * zn, xsib_ssem.at[0], xsib_rsem.at[0]).wait_send()
            all_of(2 * zn, x_ssem.at[0], x_rsem.at[0, 0, 0]).wait_send()
        both(kind, run)
        ph2_drain(kind)

    krow = yn * 16

    def make_kron():
        fetch_metric.wait()
        metric = metric_ref[...]
        gram = lax.dot_general(metric, metric, (((0,), (0,)), ((), ())), preferred_element_type=F32).astype(BF16)
        spread_c = (
            lax.broadcasted_iota(jnp.int32, (aux_n, aux_n * 16), 0)
            == (lax.broadcasted_iota(jnp.int32, (aux_n, aux_n * 16), 1) >> 4)
        ).astype(F32).astype(BF16)

        def kron_step(t, carry):
            r0 = pl.multiple_of(t * krow, krow)
            spread_r = (
                ((lax.broadcasted_iota(jnp.int32, (krow, aux_n), 0) + r0) >> 4)
                == lax.broadcasted_iota(jnp.int32, (krow, aux_n), 1)
            ).astype(F32).astype(BF16)
            rows = jnp.dot(spread_r, gram, preferred_element_type=F32).astype(BF16)
            full = jnp.dot(rows, spread_c, preferred_element_type=F32)
            same = (lax.broadcasted_iota(jnp.int32, full.shape, 0) & 15) == (
                lax.broadcasted_iota(jnp.int32, full.shape, 1) & 15)
            kron[pl.ds(r0, krow), :] = jnp.where(same, full, 0.0).astype(BF16)
            return carry

        lax.fori_loop(0, aux_n * 16 // krow, kron_step, 0)
        for u in range(UNITS):
            coeff[u, zn, 0 : bs // GRAN] = jnp.zeros((bs // GRAN, GRAN, ucol), BF16)

    def a2a_y(i, src, mid, k):
        to = wrap(y + k, yn)
        return remote(src.at[:, to], mid.at[y], a2a_ssem.at[i, 0, k], a2a_rsem.at[i, 0, k], at_y(k))

    def a2a_z(i, mid, dst, k):
        to = wrap(z + k, zn)
        return remote(mid.at[:, to], dst.at[z], a2a_ssem.at[i, 1, k], a2a_rsem.at[i, 1, k], at_z(k))

    def a2a_y_start(i, src, mid):
        for k in far_first(yn):
            a2a_y(i, src, mid, k).start()
        mid[y] = src[:, y]

    def a2a_z_start(i, src, mid, dst):
        for k in range(1, yn):
            a2a_y(i, src, mid, k).wait()
        for k in far_first(zn):
            a2a_z(i, mid, dst, k).start()
        dst[z] = mid[:, z]

    def a2a_end(i, mid, dst):
        for k in range(1, zn):
            a2a_z(i, mid, dst, k).wait()

    def scatter_arrive():
        @pl.when(bas == 0)
        def _():
            pltpu.make_async_copy(blocks_hbm, land_blocks, local_sem.at[2]).wait()
            pltpu.make_async_copy(live_hbm, land_live, local_sem.at[5]).wait()
            pltpu.make_async_copy(win_src(0), win, local_sem.at[1]).wait()

        @pl.when(bas != 0)
        def _():
            for copy in scatter(0):
                copy.wait_recv()

        win_tiles[...] = win[...].reshape(zn, yn, 16, bs)

    per_z = yn * block // bs

    def tables():
        win_tabs = [
            pltpu.make_async_copy(land_blocks, win_blocks, local_sem.at[2]),
            pltpu.make_async_copy(land_live, win_live, local_sem.at[5]),
        ]
        for copy in win_tabs:
            copy.start()
        for copy in own_tabs + win_tabs:
            copy.wait()
        wrow = (bas * ms) // bs

        def fill(s, carry):
            for b in range(nrow + 1):
                if b < nrow:
                    blk, live = own_blocks[b, s], own_live[b, s]
                else:
                    blk, live = win_blocks[wrow, s], win_live[wrow, s]
                place = live * (blk - dead) + dead
                tab_z[b, s] = lax.div(place, per_z)
                tab_o[b, s] = lax.rem(place, per_z) * (bs // GRAN)
            return carry

        lax.fori_loop(0, nz, fill, 0)

    def mix():
        def mix_step(t, carry):
            r0 = pl.multiple_of(t * krow, krow)
            rows = jnp.dot(
                kron[pl.ds(r0, krow), :], mixin[...].reshape(aux_n * 16, bs), preferred_element_type=F32)
            mixed[t] = rows.astype(BF16).reshape(yn, 16, bs)
            return carry

        lax.fori_loop(0, zn, mix_step, 0)

    def chain(k):
        if k == CHAIN[0]:
            scatter_arrive()
            a2a_y_start(0, win_tiles, mid_a)
            make_kron()
        if k == CHAIN[1]:
            a2a_z_start(0, win_tiles, mid_a, mixin)
            tables()
        if k == CHAIN[2]:
            a2a_end(0, mid_a, mixin)
            mix()
            a2a_y_start(1, mixed, mid_b)
        if k == CHAIN[3]:
            a2a_z_start(1, mixed, mid_b, imix_tiles)

    CHAIN = [min(k, 2 * far) for k in (0, 2, 4, 6)]
    own_slab()
    chain(0)
    for k in range(1, far + 1):
        arrive(PARITY, k)
        chain(2 * k - 1)
        arrive(COMMON, k)
        x_arrive(k - 1)
        chain(2 * k)
    x_arrive(far)
    a2a_end(1, mid_b, imix_tiles)
    imix[...] = imix_tiles[...].reshape(nz, ms, bs)
    fetch.wait()
    sib_arrive(PARITY)
    sib_arrive(COMMON)

    def block_of(g, b, s):
        zi, off = tab_z[b, s], tab_o[b, s]
        return jnp.concatenate(
            [coeff[2 * g + i, zi, pl.ds(off, bs // GRAN)].reshape(bs, ucol) for i in range(2)], axis=1)

    def w_step(g, carry):
        acc = jnp.zeros((ms, gcol), F32)
        for s in range(0, nz, 2):
            lhs = jnp.concatenate([imix[s], imix[s + 1]], axis=1)
            rhs = jnp.concatenate([block_of(g, nrow, s), block_of(g, nrow, s + 1)], axis=0)
            acc = acc + jnp.dot(lhs, rhs, preferred_element_type=F32)
        for hf in range(2):
            wfull[g, hf, bas] = acc[hf * mh : (hf + 1) * mh, :].astype(BF16)
        return carry

    lax.fori_loop(0, GROUPS, w_step, 0)

    def w_copy(hf, k):
        ref = wfull.at[:, hf, bas]
        return remote(ref, ref, w_ssem.at[hf, k], w_rsem.at[hf, k], at_x(k))

    def ws_copy(hf, k):
        ref = wfull.at[:, hf, wrap(x + k, xn) * 2 + c]
        return remote(ref, ref, ws_ssem.at[hf, k], ws_rsem.at[hf, k], sib)

    for hf in range(2):
        for k in far_first(xn):
            w_copy(hf, k).start()
        ws_copy(hf, 0).start()

    def w_pass_on(hf):
        for k in range(1, xn):
            w_copy(hf, k).wait()
            ws_copy(hf, xn - k).start()

    def half_step(t, carry):
        b, g = t // GROUPS, lax.rem(t, GROUPS)
        acc = jnp.zeros((bs, gcol), F32)
        for s in range(0, nz, 2):
            lhs = jnp.concatenate([ints[b, s], ints[b, s + 1]], axis=1)
            rhs = jnp.concatenate([block_of(g, b, s), block_of(g, b, s + 1)], axis=0)
            acc = acc + jnp.dot(lhs, rhs, preferred_element_type=F32)
        half[g, pl.ds(pl.multiple_of(b * bs, bs), bs), :] = acc.astype(BF16)
        return carry

    half_total = nrow * GROUPS
    lax.fori_loop(0, half_total * 4 // 5, half_step, 0)
    w_pass_on(0)
    lax.fori_loop(half_total * 4 // 5, half_total, half_step, 0)

    tn = 256 if ncol % 256 == 0 else 128

    def exch_step(hf, t, carry):
        n0 = pl.multiple_of(t * tn, tn)
        acc = jnp.zeros((krows // 2, tn), F32)
        for g in range(GROUPS):
            acc = acc + lax.dot_general(
                wfull[g, hf].reshape(krows // 2, gcol), half[g, pl.ds(n0, tn), :], (((1,), (1,)), ((), ())),
                preferred_element_type=F32)
        exch[:, pl.ds(n0, tn)] = acc
        return carry

    def rs_a(k):
        to = wrap(y + k, yn)
        return remote(send_a.at[to], recv_a.at[y], rs_ssem.at[0, k], rs_rsem.at[0, k], at_y(k))

    def rs_b(hf, k):
        to = wrap(z + k, zn)
        return remote(send_b.at[hf, to], recv_b.at[hf, z], rsb_ssem.at[hf, k], rsb_rsem.at[hf, k], at_z(k))

    def share(hf):
        lax.fori_loop(0, ncol // tn, functools.partial(exch_step, hf), 0)
        for t in range(zn):
            send_b[hf, t] = exch[t * mh : (t + 1) * mh, hcol:].astype(BF16)
        for k in far_first(zn):
            rs_b(hf, k).start()
        recv_b[hf, z] = send_b[hf, z]
        for i in range(yh):
            t = hf * yh + i
            rows = jnp.concatenate(
                [exch[zz * mh + i * out_rows : zz * mh + (i + 1) * out_rows, :hcol] for zz in range(zn)], axis=0)
            send_a[t] = rows.astype(BF16)
            pl.when(t != y)(lambda: rs_a(wrap(t - y + yn, yn)).start())

    for hf in range(2):
        if hf == 1:
            w_pass_on(1)
        for k in range(xn):
            ws_copy(hf, k).wait()
        share(hf)
    recv_a[y] = send_a[y]

    @pl.when(bas == 0)
    def _():
        for j in range(1, bas_n):
            for copy in scatter(j):
                copy.wait_send()

    gather_drain(PARITY)
    gather_drain(COMMON)

    def total(ref, n):
        acc = ref[0].astype(F32)
        for i in range(1, n):
            acc = acc + ref[i].astype(F32)
        return acc

    for k in range(1, yn):
        rs_a(k).wait()
    sum_a = total(recv_a, yn)
    for t in range(zn):
        send_a2[t] = sum_a[t * out_rows : (t + 1) * out_rows, :]

    def rs_a2(k):
        to = wrap(z + k, zn)
        return remote(send_a2.at[to], recv_a2.at[z], rs_ssem.at[2, k], rs_rsem.at[2, k], at_z(k))

    for k in far_first(zn):
        rs_a2(k).start()
    recv_a2[z] = send_a2[z]

    for hf in range(2):
        for k in range(1, zn):
            rs_b(hf, k).wait()
        sum_b = total(recv_b.at[hf], zn)
        for i in range(yh):
            send_b2[hf * yh + i] = sum_b[i * out_rows : (i + 1) * out_rows, :]

    def rs_b2(k):
        to = wrap(y + k, yn)
        return remote(send_b2.at[to], recv_b2.at[y], rs_ssem.at[3, k], rs_rsem.at[3, k], at_y(k))

    for k in far_first(yn):
        rs_b2(k).start()
    recv_b2[y] = send_b2[y]

    factor = 1.0 / math.sqrt(aux_n * occ)
    for k in range(1, zn):
        rs_a2(k).wait()
    out_ref[:, :hcol] = total(recv_a2, zn) * factor
    for k in range(1, yn):
        rs_b2(k).wait()
    out_ref[:, hcol:] = total(recv_b2, yn) * factor


def on_device(dims, integrals, coefficients, metric, pair_blocks, pair_live):
    zn, yn, xn, bs, nz, nrow, occ, krows, rows_dev, nb = dims
    bas_n, aux_n = 2 * xn, zn * yn
    block = rows_dev * bas_n
    gcol = occ // GROUPS
    ms = krows // bas_n
    out_rows = krows // aux_n
    mh = ms // 2
    assert ms == yn * out_rows
    ncol = nrow * bs
    hcol = ncol // 2
    pad = -(-rows_dev // 16) * 16
    v, dma = pltpu.VMEM, pltpu.SemaphoreType.DMA
    most = max(yn, zn)
    return pl.pallas_call(
        functools.partial(kernel, dims),
        out_shape=jax.ShapeDtypeStruct((out_rows, ncol), F32),
        in_specs=[pl.BlockSpec(memory_space=pltpu.HBM)] * 5,
        out_specs=pl.BlockSpec(memory_space=pltpu.VMEM),
        scratch_shapes=[
            v((nrow, nz, bs, bs), BF16),
            v((rows_dev, occ), BF16),
            v((aux_n, aux_n), BF16),
            v((pad, occ), F32),
            v((2, pad, occ // 2), BF16),
            v((bas_n, pad, occ // 2), BF16),
            v((block, occ // 2), F32),
            v((UNITS, zn + 1, yn * block // GRAN, GRAN, occ // UNITS), BF16),
            v((aux_n * 16, aux_n * 16), BF16),
            v((nz, ms, bs), BF16),
            v((zn, yn, 16, bs), BF16),
            v((yn, zn, 16, bs), BF16),
            v((zn, yn, 16, bs), BF16),
            v((zn, yn, 16, bs), BF16),
            v((yn, zn, 16, bs), BF16),
            v((zn, yn, 16, bs), BF16),
            v((nz, ms, bs), BF16),
            v((nrow, nz), jnp.int32),
            v((nrow, nz), jnp.int32),
            pltpu.SMEM((nrow, nz), jnp.int32),
            pltpu.SMEM((nrow, nz), jnp.int32),
            pltpu.SMEM((nrow, nz), jnp.int32),
            pltpu.SMEM((nrow, nz), jnp.int32),
            pltpu.SMEM((nrow + 1, nz), jnp.int32),
            pltpu.SMEM((nrow + 1, nz), jnp.int32),
            v((GROUPS, 2, bas_n, ms // 2, gcol), BF16),
            v((GROUPS, ncol, gcol), BF16),
            v((krows // 2, ncol), F32),
            v((yn, zn * out_rows, hcol), BF16),
            v((yn, zn * out_rows, hcol), BF16),
            v((2, zn, yn // 2 * out_rows, hcol), BF16),
            v((2, zn, yn // 2 * out_rows, hcol), BF16),
            v((zn, out_rows, hcol), F32),
            v((zn, out_rows, hcol), F32),
            v((yn, out_rows, hcol), F32),
            v((yn, out_rows, hcol), F32),
            dma((8,)),
            dma((bas_n,)), dma((bas_n,)),
            dma((bas_n, 3)), dma((3,)),
            dma((2, 2, most)), dma((2, 2, most)),
            dma((2, 2, 2)), dma((2, 2, 2, 2, most)),
            dma((2, 2)), dma((2, 2)),
            dma((1,)), dma((2, 2, most)),
            dma((1,)), dma((1,)),
            dma((2, 2, most)), dma((2, 2, most)),
            dma((2, xn)), dma((2, xn)),
            dma((2, xn)), dma((2, xn)),
            dma((4, most)), dma((4, most)),
            dma((2, most)), dma((2, most)),
        ],
        compiler_params=pltpu.CompilerParams(
            collective_id=0, has_side_effects=True, vmem_limit_bytes=52 * 1024 * 1024),
        cost_estimate=pl.CostEstimate(
            flops=2 * (nrow * nz * bs * bs * occ + krows * ncol * occ), bytes_accessed=4 * 1024 * 1024,
            transcendentals=0),
    )(integrals[0], coefficients, metric, pair_blocks, pair_live)


def solution(mesh, grid=(8, 8)):
    zn, yn = grid
    xn = mesh.shape["bas"] // 2

    def whole(integrals, coefficients, metric, pair_blocks, pair_live):
        bs, nz = integrals.shape[-1], integrals.shape[2]
        nb, occ = coefficients.shape
        nrow = integrals.shape[1] // (2 * xn)
        krows = 512 if nb == 6144 else 128
        dims = (zn, yn, xn, bs, nz, nrow, occ, krows, nb // mesh.size, nb)
        return jax.shard_map(
            functools.partial(on_device, dims),
            mesh=mesh,
            in_specs=(
                P("aux", "bas", None, None, None),
                P(("aux", "bas"), None),
                P(),
                P("bas", None),
                P("bas", None),
            ),
            out_specs=P("aux", "bas"),
            check_vma=False,
        )(integrals, coefficients, metric, pair_blocks, pair_live)

    return whole
```

```python
import functools
import math

import jax
import jax.numpy as jnp
from jax import lax
from jax.experimental import pallas as pl
from jax.experimental.pallas import tpu as pltpu
from jax.sharding import PartitionSpec as P

BF16 = jnp.bfloat16
F32 = jnp.float32
GROUPS = 4
UNITS = 8
GRAN = 16
COMMON, PARITY = 1, 0


def wrap(value, n):
    assert n & (n - 1) == 0
    return value & (n - 1)


def far_first(n):
    return sorted(range(1, n), key=lambda k: -min(k, n - k))


def kernel(
    dims,
    ints_hbm,
    coef_hbm,
    metric_hbm,
    blocks_hbm,
    live_hbm,
    out_ref,
    ints,
    coef_ref,
    metric_ref,
    raw_f32,
    raw_send,
    raw_recv,
    join_f32,
    coeff,
    kron,
    win,
    win_tiles,
    mid_a,
    mixin,
    mixed,
    mid_b,
    imix_tiles,
    imix,
    land_blocks,
    land_live,
    win_blocks,
    win_live,
    own_blocks,
    own_live,
    tab_z,
    tab_o,
    wfull,
    half,
    exch,
    send_a,
    recv_a,
    send_b,
    recv_b,
    send_a2,
    recv_a2,
    send_b2,
    recv_b2,
    local_sem,
    raw_ssem,
    raw_rsem,
    scat_ssem,
    scat_rsem,
    ph2_ssem,
    ph2_rsem,
    ring_ssem,
    ring_rsem,
    sib_ssem,
    sib_rsem,
    x_ssem,
    x_rsem,
    xsib_ssem,
    xsib_rsem,
    a2a_ssem,
    a2a_rsem,
    w_ssem,
    w_rsem,
    ws_ssem,
    ws_rsem,
    rs_ssem,
    rs_rsem,
    rsb_ssem,
    rsb_rsem,
):
    zn, yn, xn, bs, nz, nrow, occ, krows, rows_dev, nb = dims
    bas_n = 2 * xn
    aux_n = zn * yn
    block = rows_dev * bas_n
    gcol = occ // GROUPS
    ucol = occ // UNITS
    per = block // GRAN
    zh, yh = zn // 2, yn // 2
    ms = krows // bas_n
    out_rows = krows // aux_n
    mh = ms // 2
    assert ms == yn * out_rows
    ncol = nrow * bs
    hcol = ncol // 2
    dead = nb // bs

    aux = lax.axis_index("aux")
    bas = lax.axis_index("bas")
    y = wrap(aux, yn)
    z = (aux - y) // yn
    c = wrap(bas, 2)
    x = (bas - c) // 2
    par = wrap(x, 2)
    sib = (aux, x * 2 + 1 - c)

    def at_y(k):
        return (z * yn + wrap(y + k, yn), bas)

    def at_z(k):
        return (wrap(z + k, zn) * yn + y, bas)

    def at_bas(k):
        return (aux, wrap(bas + k, bas_n))

    def at_x(k):
        return (aux, wrap(x + k, xn) * 2 + c)

    def remote(src, dst, ssem, rsem, dev):
        return pltpu.make_async_remote_copy(
            src_ref=src, dst_ref=dst, send_sem=ssem, recv_sem=rsem,
            device_id=dev, device_id_type=pl.DeviceIdType.MESH)

    barrier = pltpu.get_barrier_semaphore()
    for k in range(1, yn):
        pl.semaphore_signal(barrier, inc=1, device_id=at_y(k), device_id_type=pl.DeviceIdType.MESH)
    for k in range(1, zn):
        pl.semaphore_signal(barrier, inc=1, device_id=at_z(k), device_id_type=pl.DeviceIdType.MESH)
    for k in range(1, bas_n):
        pl.semaphore_signal(barrier, inc=1, device_id=at_bas(k), device_id_type=pl.DeviceIdType.MESH)

    fetch_coef = pltpu.make_async_copy(coef_hbm, coef_ref, local_sem.at[6])
    fetch_coef.start()
    fetch_metric = pltpu.make_async_copy(metric_hbm, metric_ref, local_sem.at[7])
    fetch_metric.start()
    fetch = pltpu.make_async_copy(ints_hbm, ints, local_sem.at[0])
    fetch.start()
    own_tabs = [
        pltpu.make_async_copy(blocks_hbm, own_blocks, local_sem.at[3]),
        pltpu.make_async_copy(live_hbm, own_live, local_sem.at[4]),
    ]
    for copy in own_tabs:
        copy.start()
    raw_f32[...] = jnp.zeros_like(raw_f32)
    fetch_coef.wait()
    raw_f32[0:rows_dev, :] = coef_ref[...].astype(F32)
    packed = raw_f32[...].astype(BF16)
    raw_send[0] = packed[:, : occ // 2]
    raw_send[1] = packed[:, occ // 2 :]
    pl.semaphore_wait(barrier, yn - 1 + zn - 1 + bas_n - 1)

    def raw_copy(k):
        to = wrap(bas + k, bas_n)
        return remote(raw_send.at[wrap(to, 2)], raw_recv.at[bas], raw_ssem.at[k], raw_rsem.at[k], (aux, to))

    for k in far_first(bas_n):
        raw_copy(k).start()
    raw_recv[bas] = raw_send[c]

    def win_src(j):
        b = (j * ms) // bs
        off = (j * ms) % bs
        return ints_hbm.at[b, :, pl.ds(off, ms), :]

    def scatter(j):
        return [
            remote(blocks_hbm, land_blocks, scat_ssem.at[j, 1], scat_rsem.at[1], (aux, j)),
            remote(live_hbm, land_live, scat_ssem.at[j, 2], scat_rsem.at[2], (aux, j)),
            remote(win_src(j), win, scat_ssem.at[j, 0], scat_rsem.at[0], (aux, j)),
        ]

    @pl.when(bas == 0)
    def _():
        for j in range(1, bas_n):
            for copy in scatter(j):
                copy.start()
        pltpu.make_async_copy(blocks_hbm, land_blocks, local_sem.at[2]).start()
        pltpu.make_async_copy(live_hbm, land_live, local_sem.at[5]).start()
        pltpu.make_async_copy(win_src(0), win, local_sem.at[1]).start()

    for k in range(1, bas_n):
        raw_copy(k).wait()
    for j in range(bas_n):
        join_f32[j * rows_dev : (j + 1) * rows_dev, :] = raw_recv[j][0:rows_dev, :].astype(F32)

    def unit(st, kind):
        return 4 * c + st if kind == COMMON else 4 * c + 2 + par

    joined = join_f32[...].astype(BF16)
    cols = [joined[:, k * ucol : (k + 1) * ucol].reshape(per, GRAN, ucol) for k in range(4)]
    for st in range(2):
        coeff[unit(st, COMMON), z, pl.ds(y * per, per)] = cols[st]
    coeff[unit(0, PARITY), z, pl.ds(y * per, per)] = jnp.where(par == 0, cols[2], cols[3])

    def both(kind, run):
        if kind == COMMON:
            run(0)
            run(1)
        else:
            pl.when(c == 0)(lambda: run(0))
            pl.when(c == 1)(lambda: run(1))

    def ph2_copy(st, kind, k):
        ref = coeff.at[unit(st, kind), z, pl.ds(y * per, per)]
        return remote(
            ref, ref, ph2_ssem.at[st, kind, k], ph2_rsem.at[st, kind, k], at_z(k) if st == 0 else at_y(k))

    def near_first(n):
        return sorted(range(1, n), key=lambda k: min(k, n - k))

    def ph2_start(kind):
        def run(st):
            n = zn if st == 0 else yn
            for k in near_first(n):
                if n != 8 or min(k, n - k) <= 2:
                    ph2_copy(st, kind, k).start()
        both(kind, run)

    def ph2_relay(st, kind, k):
        n, me, at = (zn, z, at_z) if st == 0 else (yn, y, at_y)
        if n != 8 or k not in (2, n - 2):
            return
        pos = wrap(me + n - k, n)
        zz, yy = (pos, y) if st == 0 else (z, pos)
        ref = coeff.at[unit(st, kind), zz, pl.ds(yy * per, per)]
        up = (k == 2) == (st == kind)
        for far_k in ((3, 4) if k == 2 else (n - 3, n - 4)):
            if far_k == 4 and not up:
                continue
            remote(ref, ref, ph2_ssem.at[st, kind, far_k], ph2_rsem.at[st, kind, far_k], at(wrap(far_k - k + n, n))).start()

    def ph2_drain(kind):
        def run(st):
            for k in range(1, zn if st == 0 else yn):
                ph2_copy(st, kind, k).wait_send()
        both(kind, run)

    ph2_start(COMMON)
    ph2_start(PARITY)

    def half_slab(u, st, d, h, s):
        n, me = (yn, y) if st == 0 else (zn, z)
        pos = wrap(me + (n - s if d == 0 else s), n)
        if st == 0:
            return coeff.at[u, pl.ds(h * zh, zh), pl.ds(pos * per, per)]
        return coeff.at[u, pos, pl.ds(h * yh * per, yh * per)]

    far = yn // 2

    def next_at(st, d):
        n, at = (yn, at_y) if st == 0 else (zn, at_z)
        return at(1) if d == 0 else at(n - 1)

    def ring_copy(st, kind, d, h, s):
        ref = half_slab(unit(st, kind), st, d, h, s)
        return remote(ref, ref, ring_ssem.at[st, kind, d], ring_rsem.at[st, kind, d, h, s], next_at(st, d))

    def ring_block(st, kind, q):
        zz, yy = (q, y) if st == 0 else (z, q)
        ref = coeff.at[unit(st, kind), zz, pl.ds(yy * per, per)]
        h = q // (zh if st == 0 else yh)
        for d in range(2):
            copy = remote(ref, ref, ring_ssem.at[st, kind, d], ring_rsem.at[st, kind, d, h, 0], next_at(st, d))
            if far > 1:
                copy.start()
            else:
                pl.when(h == d)(copy.start)

    def sib_copy(st, kind, d, h, s):
        ref = half_slab(unit(st, kind), st, d, h, s)
        return remote(ref, ref, sib_ssem.at[st, kind], sib_rsem.at[st, kind], sib)

    def x_copy(st, d, h, s):
        ref = half_slab(unit(st, PARITY), st, d, h, s)
        return remote(ref, ref, x_ssem.at[0], x_rsem.at[d, h, s], at_x(1) if h == 0 else at_x(xn - 1))

    def xsib_copy(st, d, h, s):
        ref = half_slab(4 * c + 3 - par, st, d, h, s)
        return remote(ref, ref, xsib_ssem.at[0], xsib_rsem.at[0], sib)

    def all_of(n, ssem, rsem):
        if n == 2 * zn:
            ref = coeff.at[0, pl.ds(0, zn)]
        else:
            ref = coeff.at[0, pl.ds(0, n), pl.ds(0, yh * per)]
        return remote(ref, ref, ssem, rsem, sib)

    def halves(s):
        if s == 0:
            return [(0, 0), (0, 1)]
        return [(d, h) for h in range(2) for d in range(2) if s < far or h == d]

    def own_slab():
        for kind in (COMMON, PARITY):
            both(kind, lambda st: ring_block(st, kind, z if st == 0 else y))
        for k in near_first(yn):
            for kind in (COMMON, PARITY):
                def run(st):
                    n, me = (zn, z) if st == 0 else (yn, y)
                    ph2_copy(st, kind, k).wait_recv()
                    ph2_relay(st, kind, k)
                    ring_block(st, kind, wrap(me + n - k, n))
                both(kind, run)
        for kind in (COMMON, PARITY):
            arrive(kind, 0)

    def arrive(kind, s):
        def run(st):
            for d, h in halves(s):
                if s > 0:
                    ring_copy(st, kind, d, h, s - 1).wait_recv()
                    if s + 1 < far or (s + 1 == far and h == d):
                        ring_copy(st, kind, d, h, s).start()
                if kind == PARITY:
                    x_copy(st, d, h, s).start()
                sib_copy(st, kind, d, h, s).start()
        both(kind, run)

    def x_arrive(s):
        def run(st):
            for d, h in halves(s):
                x_copy(st, d, h, s).wait_recv()
                xsib_copy(st, d, h, s).start()
        both(PARITY, run)

    def sib_arrive(kind):
        def run(st):
            all_of(2 * zn, sib_ssem.at[st, kind], sib_rsem.at[st, kind]).wait_recv()
        if kind == COMMON:
            run(0)
            run(1)
        else:
            pl.when(c == 1)(lambda: run(0))
            pl.when(c == 0)(lambda: run(1))
            all_of(2 * zn, xsib_ssem.at[0], xsib_rsem.at[0]).wait_recv()

    def gather_drain(kind):
        def run(st):
            all_of(2 * zn, sib_ssem.at[st, kind], sib_rsem.at[st, kind]).wait_send()
            for d in range(2):
                all_of(yn - 1, ring_ssem.at[st, kind, d], ring_rsem.at[st, kind, d, 0, 0]).wait_send()
        if kind == PARITY:
            all_of(2 * zn, xsib_ssem.at[0], xsib_rsem.at[0]).wait_send()
            all_of(2 * zn, x_ssem.at[0], x_rsem.at[0, 0, 0]).wait_send()
        both(kind, run)
        ph2_drain(kind)

    krow = yn * 16

    def make_kron():
        fetch_metric.wait()
        metric = metric_ref[...]
        gram = lax.dot_general(metric, metric, (((0,), (0,)), ((), ())), preferred_element_type=F32).astype(BF16)
        spread_c = (
            lax.broadcasted_iota(jnp.int32, (aux_n, aux_n * 16), 0)
            == (lax.broadcasted_iota(jnp.int32, (aux_n, aux_n * 16), 1) >> 4)
        ).astype(F32).astype(BF16)

        def kron_step(t, carry):
            r0 = pl.multiple_of(t * krow, krow)
            spread_r = (
                ((lax.broadcasted_iota(jnp.int32, (krow, aux_n), 0) + r0) >> 4)
                == lax.broadcasted_iota(jnp.int32, (krow, aux_n), 1)
            ).astype(F32).astype(BF16)
            rows = jnp.dot(spread_r, gram, preferred_element_type=F32).astype(BF16)
            full = jnp.dot(rows, spread_c, preferred_element_type=F32)
            same = (lax.broadcasted_iota(jnp.int32, full.shape, 0) & 15) == (
                lax.broadcasted_iota(jnp.int32, full.shape, 1) & 15)
            kron[pl.ds(r0, krow), :] = jnp.where(same, full, 0.0).astype(BF16)
            return carry

        lax.fori_loop(0, aux_n * 16 // krow, kron_step, 0)
        for u in range(UNITS):
            coeff[u, zn, 0 : bs // GRAN] = jnp.zeros((bs // GRAN, GRAN, ucol), BF16)

    def a2a_y(i, src, mid, k):
        to = wrap(y + k, yn)
        return remote(src.at[:, to], mid.at[y], a2a_ssem.at[i, 0, k], a2a_rsem.at[i, 0, k], at_y(k))

    def a2a_z(i, mid, dst, k):
        to = wrap(z + k, zn)
        return remote(mid.at[:, to], dst.at[z], a2a_ssem.at[i, 1, k], a2a_rsem.at[i, 1, k], at_z(k))

    def a2a_y_start(i, src, mid):
        for k in far_first(yn):
            a2a_y(i, src, mid, k).start()
        mid[y] = src[:, y]

    def a2a_z_start(i, src, mid, dst):
        for k in range(1, yn):
            a2a_y(i, src, mid, k).wait()
        for k in far_first(zn):
            a2a_z(i, mid, dst, k).start()
        dst[z] = mid[:, z]

    def a2a_end(i, mid, dst):
        for k in range(1, zn):
            a2a_z(i, mid, dst, k).wait()

    def scatter_arrive():
        @pl.when(bas == 0)
        def _():
            pltpu.make_async_copy(blocks_hbm, land_blocks, local_sem.at[2]).wait()
            pltpu.make_async_copy(live_hbm, land_live, local_sem.at[5]).wait()
            pltpu.make_async_copy(win_src(0), win, local_sem.at[1]).wait()

        @pl.when(bas != 0)
        def _():
            for copy in scatter(0):
                copy.wait_recv()

        win_tiles[...] = win[...].reshape(zn, yn, 16, bs)

    per_z = yn * block // bs

    def tables():
        win_tabs = [
            pltpu.make_async_copy(land_blocks, win_blocks, local_sem.at[2]),
            pltpu.make_async_copy(land_live, win_live, local_sem.at[5]),
        ]
        for copy in win_tabs:
            copy.start()
        for copy in own_tabs + win_tabs:
            copy.wait()
        wrow = (bas * ms) // bs

        def fill(s, carry):
            for b in range(nrow + 1):
                if b < nrow:
                    blk, live = own_blocks[b, s], own_live[b, s]
                else:
                    blk, live = win_blocks[wrow, s], win_live[wrow, s]
                place = live * (blk - dead) + dead
                tab_z[b, s] = lax.div(place, per_z)
                tab_o[b, s] = lax.rem(place, per_z) * (bs // GRAN)
            return carry

        lax.fori_loop(0, nz, fill, 0)

    def mix():
        def mix_step(t, carry):
            r0 = pl.multiple_of(t * krow, krow)
            rows = jnp.dot(
                kron[pl.ds(r0, krow), :], mixin[...].reshape(aux_n * 16, bs), preferred_element_type=F32)
            mixed[t] = rows.astype(BF16).reshape(yn, 16, bs)
            return carry

        lax.fori_loop(0, zn, mix_step, 0)

    def chain(k):
        if k == CHAIN[0]:
            scatter_arrive()
            a2a_y_start(0, win_tiles, mid_a)
            make_kron()
        if k == CHAIN[1]:
            a2a_z_start(0, win_tiles, mid_a, mixin)
            tables()
        if k == CHAIN[2]:
            a2a_end(0, mid_a, mixin)
            mix()
            a2a_y_start(1, mixed, mid_b)
        if k == CHAIN[3]:
            a2a_z_start(1, mixed, mid_b, imix_tiles)

    CHAIN = [min(k, 2 * far) for k in (0, 2, 4, 6)]
    own_slab()
    chain(0)
    for k in range(1, far + 1):
        arrive(PARITY, k)
        chain(2 * k - 1)
        arrive(COMMON, k)
        x_arrive(k - 1)
        chain(2 * k)
    x_arrive(far)
    a2a_end(1, mid_b, imix_tiles)
    imix[...] = imix_tiles[...].reshape(nz, ms, bs)
    fetch.wait()
    sib_arrive(PARITY)
    sib_arrive(COMMON)

    def block_of(g, b, s):
        zi, off = tab_z[b, s], tab_o[b, s]
        return jnp.concatenate(
            [coeff[2 * g + i, zi, pl.ds(off, bs // GRAN)].reshape(bs, ucol) for i in range(2)], axis=1)

    def w_step(g, carry):
        acc = jnp.zeros((ms, gcol), F32)
        for s in range(0, nz, 2):
            lhs = jnp.concatenate([imix[s], imix[s + 1]], axis=1)
            rhs = jnp.concatenate([block_of(g, nrow, s), block_of(g, nrow, s + 1)], axis=0)
            acc = acc + jnp.dot(lhs, rhs, preferred_element_type=F32)
        for hf in range(2):
            wfull[g, hf, bas] = acc[hf * mh : (hf + 1) * mh, :].astype(BF16)
        return carry

    lax.fori_loop(0, GROUPS, w_step, 0)

    def w_copy(hf, k):
        ref = wfull.at[:, hf, bas]
        return remote(ref, ref, w_ssem.at[hf, k], w_rsem.at[hf, k], at_x(k))

    def ws_copy(hf, k):
        ref = wfull.at[:, hf, wrap(x + k, xn) * 2 + c]
        return remote(ref, ref, ws_ssem.at[hf, k], ws_rsem.at[hf, k], sib)

    for hf in range(2):
        for k in far_first(xn):
            w_copy(hf, k).start()
        ws_copy(hf, 0).start()

    def w_pass_on(hf):
        for k in range(1, xn):
            w_copy(hf, k).wait()
            ws_copy(hf, xn - k).start()

    def half_step(t, carry):
        b, g = t // GROUPS, lax.rem(t, GROUPS)
        acc = jnp.zeros((bs, gcol), F32)
        for s in range(0, nz, 2):
            lhs = jnp.concatenate([ints[b, s], ints[b, s + 1]], axis=1)
            rhs = jnp.concatenate([block_of(g, b, s), block_of(g, b, s + 1)], axis=0)
            acc = acc + jnp.dot(lhs, rhs, preferred_element_type=F32)
        half[g, pl.ds(pl.multiple_of(b * bs, bs), bs), :] = acc.astype(BF16)
        return carry

    half_total = nrow * GROUPS
    lax.fori_loop(0, half_total * 4 // 5, half_step, 0)
    w_pass_on(0)
    lax.fori_loop(half_total * 4 // 5, half_total, half_step, 0)

    tn = 256 if ncol % 256 == 0 else 128

    def exch_step(hf, t, carry):
        n0 = pl.multiple_of(t * tn, tn)
        acc = jnp.zeros((krows // 2, tn), F32)
        for g in range(GROUPS):
            acc = acc + lax.dot_general(
                wfull[g, hf].reshape(krows // 2, gcol), half[g, pl.ds(n0, tn), :], (((1,), (1,)), ((), ())),
                preferred_element_type=F32)
        exch[:, pl.ds(n0, tn)] = acc
        return carry

    def rs_a(k):
        to = wrap(y + k, yn)
        return remote(send_a.at[to], recv_a.at[y], rs_ssem.at[0, k], rs_rsem.at[0, k], at_y(k))

    def rs_b(hf, k):
        to = wrap(z + k, zn)
        return remote(send_b.at[hf, to], recv_b.at[hf, z], rsb_ssem.at[hf, k], rsb_rsem.at[hf, k], at_z(k))

    def share(hf):
        lax.fori_loop(0, ncol // tn, functools.partial(exch_step, hf), 0)
        for t in range(zn):
            send_b[hf, t] = exch[t * mh : (t + 1) * mh, hcol:].astype(BF16)
        for k in far_first(zn):
            rs_b(hf, k).start()
        recv_b[hf, z] = send_b[hf, z]
        for i in range(yh):
            t = hf * yh + i
            rows = jnp.concatenate(
                [exch[zz * mh + i * out_rows : zz * mh + (i + 1) * out_rows, :hcol] for zz in range(zn)], axis=0)
            send_a[t] = rows.astype(BF16)
            pl.when(t != y)(lambda: rs_a(wrap(t - y + yn, yn)).start())

    for hf in range(2):
        if hf == 1:
            w_pass_on(1)
        for k in range(xn):
            ws_copy(hf, k).wait()
        share(hf)
    recv_a[y] = send_a[y]

    @pl.when(bas == 0)
    def _():
        for j in range(1, bas_n):
            for copy in scatter(j):
                copy.wait_send()

    gather_drain(PARITY)
    gather_drain(COMMON)

    def total(ref, n):
        acc = ref[0].astype(F32)
        for i in range(1, n):
            acc = acc + ref[i].astype(F32)
        return acc

    for k in range(1, yn):
        rs_a(k).wait()
    sum_a = total(recv_a, yn)
    for t in range(zn):
        send_a2[t] = sum_a[t * out_rows : (t + 1) * out_rows, :]

    def rs_a2(k):
        to = wrap(z + k, zn)
        return remote(send_a2.at[to], recv_a2.at[z], rs_ssem.at[2, k], rs_rsem.at[2, k], at_z(k))

    for k in far_first(zn):
        rs_a2(k).start()
    recv_a2[z] = send_a2[z]

    for hf in range(2):
        for k in range(1, zn):
            rs_b(hf, k).wait()
        sum_b = total(recv_b.at[hf], zn)
        for i in range(yh):
            send_b2[hf * yh + i] = sum_b[i * out_rows : (i + 1) * out_rows, :]

    def rs_b2(k):
        to = wrap(y + k, yn)
        return remote(send_b2.at[to], recv_b2.at[y], rs_ssem.at[3, k], rs_rsem.at[3, k], at_y(k))

    for k in far_first(yn):
        rs_b2(k).start()
    recv_b2[y] = send_b2[y]

    factor = 1.0 / math.sqrt(aux_n * occ)
    for k in range(1, zn):
        rs_a2(k).wait()
    out_ref[:, :hcol] = total(recv_a2, zn) * factor
    for k in range(1, yn):
        rs_b2(k).wait()
    out_ref[:, hcol:] = total(recv_b2, yn) * factor


def on_device(dims, integrals, coefficients, metric, pair_blocks, pair_live):
    zn, yn, xn, bs, nz, nrow, occ, krows, rows_dev, nb = dims
    bas_n, aux_n = 2 * xn, zn * yn
    block = rows_dev * bas_n
    gcol = occ // GROUPS
    ms = krows // bas_n
    out_rows = krows // aux_n
    mh = ms // 2
    assert ms == yn * out_rows
    ncol = nrow * bs
    hcol = ncol // 2
    pad = -(-rows_dev // 16) * 16
    v, dma = pltpu.VMEM, pltpu.SemaphoreType.DMA
    most = max(yn, zn)
    return pl.pallas_call(
        functools.partial(kernel, dims),
        out_shape=jax.ShapeDtypeStruct((out_rows, ncol), F32),
        in_specs=[pl.BlockSpec(memory_space=pltpu.HBM)] * 5,
        out_specs=pl.BlockSpec(memory_space=pltpu.VMEM),
        scratch_shapes=[
            v((nrow, nz, bs, bs), BF16),
            v((rows_dev, occ), BF16),
            v((aux_n, aux_n), BF16),
            v((pad, occ), F32),
            v((2, pad, occ // 2), BF16),
            v((bas_n, pad, occ // 2), BF16),
            v((block, occ // 2), F32),
            v((UNITS, zn + 1, yn * block // GRAN, GRAN, occ // UNITS), BF16),
            v((aux_n * 16, aux_n * 16), BF16),
            v((nz, ms, bs), BF16),
            v((zn, yn, 16, bs), BF16),
            v((yn, zn, 16, bs), BF16),
            v((zn, yn, 16, bs), BF16),
            v((zn, yn, 16, bs), BF16),
            v((yn, zn, 16, bs), BF16),
            v((zn, yn, 16, bs), BF16),
            v((nz, ms, bs), BF16),
            v((nrow, nz), jnp.int32),
            v((nrow, nz), jnp.int32),
            pltpu.SMEM((nrow, nz), jnp.int32),
            pltpu.SMEM((nrow, nz), jnp.int32),
            pltpu.SMEM((nrow, nz), jnp.int32),
            pltpu.SMEM((nrow, nz), jnp.int32),
            pltpu.SMEM((nrow + 1, nz), jnp.int32),
            pltpu.SMEM((nrow + 1, nz), jnp.int32),
            v((GROUPS, 2, bas_n, ms // 2, gcol), BF16),
            v((GROUPS, ncol, gcol), BF16),
            v((krows // 2, ncol), F32),
            v((yn, zn * out_rows, hcol), BF16),
            v((yn, zn * out_rows, hcol), BF16),
            v((2, zn, yn // 2 * out_rows, hcol), BF16),
            v((2, zn, yn // 2 * out_rows, hcol), BF16),
            v((zn, out_rows, hcol), F32),
            v((zn, out_rows, hcol), F32),
            v((yn, out_rows, hcol), F32),
            v((yn, out_rows, hcol), F32),
            dma((8,)),
            dma((bas_n,)), dma((bas_n,)),
            dma((bas_n, 3)), dma((3,)),
            dma((2, 2, most)), dma((2, 2, most)),
            dma((2, 2, 2)), dma((2, 2, 2, 2, most)),
            dma((2, 2)), dma((2, 2)),
            dma((1,)), dma((2, 2, most)),
            dma((1,)), dma((1,)),
            dma((2, 2, most)), dma((2, 2, most)),
            dma((2, xn)), dma((2, xn)),
            dma((2, xn)), dma((2, xn)),
            dma((4, most)), dma((4, most)),
            dma((2, most)), dma((2, most)),
        ],
        compiler_params=pltpu.CompilerParams(
            collective_id=0, has_side_effects=True, vmem_limit_bytes=52 * 1024 * 1024),
        cost_estimate=pl.CostEstimate(
            flops=2 * (nrow * nz * bs * bs * occ + krows * ncol * occ), bytes_accessed=4 * 1024 * 1024,
            transcendentals=0),
    )(integrals[0], coefficients, metric, pair_blocks, pair_live)


def solution(mesh, grid=(8, 8)):
    zn, yn = grid
    xn = mesh.shape["bas"] // 2

    def whole(integrals, coefficients, metric, pair_blocks, pair_live):
        bs, nz = integrals.shape[-1], integrals.shape[2]
        nb, occ = coefficients.shape
        nrow = integrals.shape[1] // (2 * xn)
        krows = 512 if nb == 6144 else 128
        dims = (zn, yn, xn, bs, nz, nrow, occ, krows, nb // mesh.size, nb)
        return jax.shard_map(
            functools.partial(on_device, dims),
            mesh=mesh,
            in_specs=(
                P("aux", "bas", None, None, None),
                P(("aux", "bas"), None),
                P(),
                P("bas", None),
                P("bas", None),
            ),
            out_specs=P("aux", "bas"),
            check_vma=False,
        )(integrals, coefficients, metric, pair_blocks, pair_live)

    return whole
```
